512 devices in a mesh: row: 32 (over z, x), col: 16 (over y, core).
Axes of the slice: x: 4, y: 8, z: 8, core: 2. Of those that a mesh axis runs over, the one named last changes fastest.
Arguments:
- tokens: bfloat16 [4096, 6144], P('row', 'col'), may hold values from -6 to 6
- cotangent: bfloat16 [4096, 6144], P('row', 'col'), may hold values from -6 to 6
- w1_blocks: bfloat16 [32, 16, 2, 64, 64], P('row', 'col'), may hold values from -0.5 to 0.5
- w1_coords: int32 [32, 16, 2, 2], P('row', 'col'), may hold values from 0 to 23, as said below
- w1_count: int32 [32, 16], P('row', 'col'), may hold values from 1 to 2, as said below
- w2_blocks: bfloat16 [32, 16, 2, 64, 64], P('row', 'col'), may hold values from -0.5 to 0.5
- w2_coords: int32 [32, 16, 2, 2], P('row', 'col'), may hold values from 0 to 23, as said below
- w2_count: int32 [32, 16], P('row', 'col'), may hold values from 1 to 2, as said below
Outputs:
- input_grad: float32 [4096, 6144], P('row', 'col')
- w1_grad: float32 [32, 16, 2, 64, 64], P('row', 'col')
- w2_grad: float32 [32, 16, 2, 64, 64], P('row', 'col')
The draws below stay inside these ranges and needn't reach their ends.
Inputs may be any that keep to these rules, and one draw needn't show every extreme that they name: `w1_coords`: the 2 coordinate pairs of a tile are distinct blocks inside that tile; only the first w1_count of them are live. `w1_count`: some tile has all 2 slots live in every draw. `w2_coords`: the 2 coordinate pairs of a tile are distinct blocks inside that tile; only the first w2_count of them are live. `w2_count`: some tile has all 2 slots live in every draw.
All inputs are finite; a program needn't handle non-finite values.
Results may differ from the reference program's by a relative error of at most 0.019.
Values may be sent and summed in bfloat16 or wider, within the bound.
A program may use at most 64 MiB of HBM per device.

```python
import math
import jax
import jax.numpy as jnp
from jax import lax

D = 6144
FF = 24576
BLK = 64
CAP = 2
TOK_DEV = 128
TOKENS = 4096
DROW = 192
FCOL = 1536
N_ROW = 32
N_COL = 16


def tile_coords(key, band_rows, band_cols):
    total = band_rows * band_cols
    keys = jax.random.split(key, N_ROW * N_COL)
    picks = jax.vmap(lambda single: jax.random.permutation(single, total)[:CAP])(keys)
    chosen = jax.random.randint(jax.random.fold_in(key, 7), (), 0, N_ROW * N_COL, dtype=jnp.int32)
    shift = jnp.where(jnp.arange(N_ROW * N_COL, dtype=jnp.int32) == chosen, total - 1 - picks[:, 0], 0)
    picks = (picks + shift[:, None]) % total
    stacked = jnp.stack([picks // band_cols, picks % band_cols], axis=-1).astype(jnp.int32)
    return stacked.reshape(N_ROW, N_COL, CAP, 2)


def tile_counts(key):
    counts = jax.random.randint(key, (N_ROW * N_COL,), 1, CAP + 1, dtype=jnp.int32)
    chosen = jax.random.randint(jax.random.fold_in(key, 5), (), 0, N_ROW * N_COL, dtype=jnp.int32)
    counts = jnp.where(jnp.arange(N_ROW * N_COL, dtype=jnp.int32) == chosen, CAP, counts)
    return counts.reshape(N_ROW, N_COL).astype(jnp.int32)


def draw_w1_coords(key, part):
    key = jax.random.fold_in(key, 11)
    return tile_coords(key, D // N_ROW // BLK, FF // N_COL // BLK)


def draw_w2_coords(key, part):
    key = jax.random.fold_in(key, 12)
    return tile_coords(key, FF // N_COL // BLK, D // N_ROW // BLK)


def draw_w1_count(key, part):
    key = jax.random.fold_in(key, 13)
    return tile_counts(key)


def draw_w2_count(key, part):
    key = jax.random.fold_in(key, 14)
    return tile_counts(key)


def spiked(drawn, own_key, source, target, shards_of, factor):
    owner, partner = [(jnp.arange(drawn.shape[dim]) // (drawn.shape[dim] // shards_of)).reshape([-1 if axis == dim else 1 for axis in range(drawn.ndim)]) for dim in (source, target)]
    chosen = jax.random.permutation(own_key, shards_of)[partner]
    strong = (owner == chosen) | (owner == (partner + shards_of // 2) % shards_of)
    return jnp.where(strong, factor * drawn, drawn)


def level_of(key, extent, cuts, low, high):
    loudness = 1.0
    for dim, parts in cuts:
        heights = jax.random.uniform(jax.random.fold_in(jax.random.fold_in(key, 6), dim), (parts,), jnp.float32, low / len(cuts), high / len(cuts))
        loudness = loudness * jnp.repeat(jnp.exp(heights), extent[dim] // parts).reshape((-1,) + (1,) * (len(extent) - 1 - dim))
    return loudness


def scatter_about(rng, extent, width, reach, pieces=(), kind=jnp.bfloat16):
    result = width * jax.random.normal(rng, extent, jnp.float32)
    if pieces:
        result = result * level_of(rng, extent, pieces, -0.22, 0.18)
    return jnp.clip(result, -reach, reach).astype(kind)


def bell_draw_with(own_key, dims, width, reach, shards, heavy, kind=jnp.bfloat16):
    values = width * jax.random.normal(own_key, dims, jnp.float32)
    if shards:
        values = values * level_of(own_key, dims, shards, -0.22, 0.18)
    return jnp.clip(spiked(values, jax.random.fold_in(own_key, 3), *heavy), -reach, reach).astype(kind)


def setup_inputs(seed: int = 0) -> dict:
    splits = jax.random.split(jax.random.key(seed), 9)
    tokens = bell_draw_with(splits[0], (TOKENS, D), 1.0, 6.0, ((0, 32), (1, 16)), (0, 1, 32, 2.75))
    cotangent = bell_draw_with(splits[1], (TOKENS, D), 1.0, 6.0, ((0, 32), (1, 16)), (0, 1, 32, 2.75))
    w1_blocks = scatter_about(splits[2], (N_ROW, N_COL, CAP, BLK, BLK), (BLK * max(1, N_ROW * CAP // (FF // N_COL // BLK))) ** -0.5, 0.5, ((0, 32), (1, 16)))
    w1_coords = draw_w1_coords(jax.random.fold_in(splits[8], 71), 0)
    w1_count = draw_w1_count(jax.random.fold_in(splits[8], 71), 0)
    w2_blocks = scatter_about(splits[5], (N_ROW, N_COL, CAP, BLK, BLK), (BLK * max(1, N_ROW * CAP // (FF // N_COL // BLK))) ** -0.5, 0.5, ((0, 32), (1, 16)))
    w2_coords = draw_w2_coords(jax.random.fold_in(splits[8], 71), 0)
    w2_count = draw_w2_count(jax.random.fold_in(splits[8], 71), 0)
    return dict(tokens=tokens, cotangent=cotangent, w1_blocks=w1_blocks, w1_coords=w1_coords, w1_count=w1_count, w2_blocks=w2_blocks, w2_coords=w2_coords, w2_count=w2_count)


def gelu_pair(hidden):
    inner = 0.7978845608028654 * (hidden + 0.044715 * hidden * hidden * hidden)
    tanh_term = jnp.tanh(inner)
    gelu_out = 0.5 * hidden * (1.0 + tanh_term)
    gelu_slope = 0.5 * (1.0 + tanh_term) + 0.5 * hidden * (1.0 - tanh_term * tanh_term) * 0.7978845608028654 * (1.0 + 3.0 * 0.044715 * hidden * hidden)
    return (gelu_out, gelu_slope)

def place_blocks(products, block_index, out_blocks):
    onehot = (block_index[:, None] == jnp.arange(out_blocks, dtype=jnp.int32)[None, :]).astype(jnp.float32)
    placed = jnp.einsum('ntc,nf->tfc', products, onehot, precision=lax.Precision.HIGHEST)
    return placed.reshape(products.shape[1], out_blocks * products.shape[2])

def pick_blocks(operand, block_index):
    return jnp.take(operand.reshape(operand.shape[0], -1, BLK), block_index, axis=1).astype(jnp.float32)

def round_trip(values):
    return lax.optimization_barrier(values.astype(jnp.bfloat16)).astype(jnp.float32)

def reference(tokens, cotangent, w1_blocks, w1_coords, w1_count, w2_blocks, w2_coords, w2_count):
    row_band = DROW // BLK
    col_band = FCOL // BLK
    tile_index = jnp.repeat(jnp.arange(N_ROW, dtype=jnp.int32), CAP)
    slot_index = jnp.tile(jnp.arange(CAP, dtype=jnp.int32), N_ROW)
    highest = lax.Precision.HIGHEST

    def column_step(carried, column):
        blocks_one = lax.dynamic_index_in_dim(w1_blocks, column, 1, keepdims=False).reshape(-1, BLK, BLK).astype(jnp.float32)
        coords_one = lax.dynamic_index_in_dim(w1_coords, column, 1, keepdims=False).reshape(-1, 2)
        live_one = (slot_index < jnp.repeat(lax.dynamic_index_in_dim(w1_count, column, 1, keepdims=False), CAP)).astype(jnp.float32)
        blocks_two = lax.dynamic_index_in_dim(w2_blocks, column, 1, keepdims=False).reshape(-1, BLK, BLK).astype(jnp.float32)
        coords_two = lax.dynamic_index_in_dim(w2_coords, column, 1, keepdims=False).reshape(-1, 2)
        live_two = (slot_index < jnp.repeat(lax.dynamic_index_in_dim(w2_count, column, 1, keepdims=False), CAP)).astype(jnp.float32)
        model_one = tile_index * row_band + coords_one[:, 0]
        hidden_one = coords_one[:, 1]
        hidden_two = coords_two[:, 0]
        model_two = tile_index * row_band + coords_two[:, 1]
        feat_blocks = pick_blocks(tokens, model_one)
        pre_blocks = jnp.einsum('tnb,nbc->ntc', feat_blocks, blocks_one, precision=highest) * live_one[:, None, None]
        hidden = place_blocks(pre_blocks, hidden_one, col_band)
        gelu_out, gelu_slope = gelu_pair(hidden)
        active = gelu_out.astype(jnp.bfloat16)
        up_blocks = pick_blocks(cotangent, model_two)
        back_blocks = jnp.einsum('tnc,nbc->ntb', up_blocks, blocks_two, precision=highest) * live_two[:, None, None]
        upstream = place_blocks(back_blocks, hidden_two, col_band)
        hidden_grad = (upstream * gelu_slope).astype(jnp.bfloat16)
        grad_blocks = pick_blocks(hidden_grad, hidden_one)
        back_one = jnp.einsum('tnc,nbc->ntb', grad_blocks, blocks_one, precision=highest) * live_one[:, None, None]
        partial_input = place_blocks(back_one, model_one, D // BLK)
        carried = carried + round_trip(partial_input)
        feat_groups = feat_blocks.reshape(N_ROW, TOK_DEV, -1, BLK)
        grad_groups = grad_blocks.reshape(N_ROW, TOK_DEV, -1, BLK)
        terms_one = jnp.einsum('gtnb,gtnc->gnbc', feat_groups, grad_groups, precision=highest)
        total_one = lax.optimization_barrier(jnp.sum(round_trip(terms_one), axis=0)) * live_one[:, None, None]
        act_groups = pick_blocks(active, hidden_two).reshape(N_ROW, TOK_DEV, -1, BLK)
        up_groups = up_blocks.reshape(N_ROW, TOK_DEV, -1, BLK)
        terms_two = jnp.einsum('gtnb,gtnc->gnbc', act_groups, up_groups, precision=highest)
        total_two = lax.optimization_barrier(jnp.sum(round_trip(terms_two), axis=0)) * live_two[:, None, None]
        return (carried, (total_one.reshape(N_ROW, CAP, BLK, BLK), total_two.reshape(N_ROW, CAP, BLK, BLK)))
    start_carry = jnp.zeros((TOKENS, D), jnp.float32)
    input_grad, stacked = lax.scan(column_step, start_carry, jnp.arange(N_COL, dtype=jnp.int32))
    grad_scale = 1.0 / math.sqrt(TOKENS)
    w1_grad = jnp.transpose(stacked[0], (1, 0, 2, 3, 4)) * grad_scale
    w2_grad = jnp.transpose(stacked[1], (1, 0, 2, 3, 4)) * grad_scale
    return (input_grad, w1_grad, w2_grad)
```

```python
import functools
import math

import jax
import jax.numpy as jnp
from jax import lax
from jax.experimental import pallas as pl
from jax.experimental.pallas import tpu as pltpu
from jax.sharding import PartitionSpec as P

MESH = pl.DeviceIdType.MESH
F32 = jnp.float32
BF16 = jnp.bfloat16
NT = (((1,), (1,)), ((), ()))
NN = (((1,), (0,)), ((), ()))
TN = (((0,), (0,)), ((), ()))
NZ, NX, NY = 8, 4, 8
BLK = 64
DEAD = -64

FAMILIES = (
    ("right", 8), ("left", 8), ("pair", 16), ("wx", 3), ("mx", 3), ("wzr", 4), ("wzl", 4),
    ("mzr", 4), ("mzl", 3), ("part", 8), ("cr", 4), ("cl", 4), ("gx", 24), ("gz", 7),
)
BASE = {}
TOTAL = 0
for family, amount in FAMILIES:
    BASE[family] = TOTAL
    TOTAL += amount


def gelu_pair(hidden):
    inner = 0.7978845608028654 * (hidden + 0.044715 * hidden * hidden * hidden)
    tanh_term = jnp.tanh(inner)
    gelu_out = 0.5 * hidden * (1.0 + tanh_term)
    gelu_slope = 0.5 * (1.0 + tanh_term) + 0.5 * hidden * (
        1.0 - tanh_term * tanh_term
    ) * 0.7978845608028654 * (1.0 + 3.0 * 0.044715 * hidden * hidden)
    return (gelu_out, gelu_slope)


def kernel(
    scale, tok, cot, wpk, meta, ig, wg,
    xc, wall, mall, a1, a2, hid, ups, act, grd, part, psib, ssum, rbr, rbl,
    gr, xr, zs, zr, mv, dv, ms, md, send_sems, recv_sems, local_sems,
):
    row, col = lax.axis_index("row"), lax.axis_index("col")
    z, x, y, core = row // NX, row % NX, col // 2, col % 2

    def dev(dz=0, dx=0, dy=0, other=False):
        there = (1 - core) if other else core
        return ((z + dz) % NZ * NX + (x + dx) % NX, (y + dy) % NY * 2 + there)

    sibling = dev(other=True)
    right, left = dev(dy=1), dev(dy=NY - 1)
    z_right, z_left = dev(dz=1), dev(dz=NZ - 1)

    barrier = pltpu.get_barrier_semaphore()
    partners = [sibling, right, left]
    partners += [dev(dx=e) for e in range(1, NX)]
    partners += [dev(dz=e) for e in range(1, NZ)]
    for partner in partners:
        pl.semaphore_signal(barrier, inc=1, device_id=partner, device_id_type=MESH)

    pending = []

    def describe(family, n, src, dst, target):
        slot = BASE[family] + n
        return pltpu.make_async_remote_copy(
            src_ref=src, dst_ref=dst, send_sem=send_sems.at[slot], recv_sem=recv_sems.at[slot],
            device_id=target, device_id_type=MESH,
        )

    def send(family, n, src, dst, target):
        copy = describe(family, n, src, dst, target)
        copy.start()
        pending.append(copy)

    def arrived(family, n, dst):
        describe(family, n, dst, dst, sibling).wait_recv()

    def shard(dy, other=False):
        return (y + dy) % NY * 2 + ((1 - core) if other else core)

    own = (tok, cot)
    xc[col, 0] = tok[...]
    xc[col, 1] = cot[...]
    wall[z, x] = wpk[...]
    mall[row] = meta[...]
    hid[0] = jnp.zeros((BLK, 128), F32)
    ups[0] = jnp.zeros((BLK, 128), F32)
    pl.semaphore_wait(barrier, len(partners))

    for e in range(1, NX):
        send("mx", e - 1, meta, mall.at[row], dev(dx=e))
        send("wx", e - 1, wpk, wall.at[z, x], dev(dx=e))
    for j in range(2):
        send("right", j, own[j], xc.at[col, j], right)
        send("left", j, own[j], xc.at[col, j], left)
    for j in range(2):
        send("pair", j, own[j], xc.at[col, j], sibling)
    for e in range(1, NX):
        there = (x + NX - e) % NX
        arrived("mx", e - 1, mall.at[z * NX + there])
        arrived("wx", e - 1, wall.at[z, there])

    def plane(dz):
        return (z + dz) % NZ

    def tiles_on(d):
        back, ahead = plane(NZ - d + 1), plane(d - 1)
        if d <= 3:
            send("mzr", d - 1, mall.at[pl.ds(back * NX, NX)], mall.at[pl.ds(back * NX, NX)], z_right)
            send("mzl", d - 1, mall.at[pl.ds(ahead * NX, NX)], mall.at[pl.ds(ahead * NX, NX)], z_left)
            send("wzr", d - 1, wall.at[back], wall.at[back], z_right)
            send("wzl", d - 1, wall.at[ahead], wall.at[ahead], z_left)
        else:
            send("mzr", d - 1, mall.at[pl.ds(back * NX, NX)], mall.at[pl.ds(back * NX, NX)], z_right)
            send("wzr", d - 1, wall.at[back, pl.ds(0, 2)], wall.at[back, pl.ds(0, 2)], z_right)
            send("wzl", d - 1, wall.at[ahead, pl.ds(2, 2)], wall.at[ahead, pl.ds(2, 2)], z_left)

    def tiles_in(d):
        back, ahead = plane(NZ - d), plane(d)
        arrived("mzr", d - 1, mall.at[pl.ds(back * NX, NX)])
        if d <= 3:
            arrived("mzl", d - 1, mall.at[pl.ds(ahead * NX, NX)])
            arrived("wzr", d - 1, wall.at[back])
            arrived("wzl", d - 1, wall.at[ahead])
            tiles_on(d + 1)
        else:
            arrived("wzr", d - 1, wall.at[back, pl.ds(0, 2)])
            arrived("wzl", d - 1, wall.at[ahead, pl.ds(2, 2)])

    def acts_in(d, j):
        if d <= 3 or j == 0:
            here = xc.at[shard(NY - d), j]
            arrived("right", 2 * (d - 1) + j, here)
            if d < 3 or (d == 3 and j == 0):
                send("right", 2 * d + j, here, here, right)
            send("pair", 2 * (NY - d) + j, here, here, sibling)
        if d <= 3 or j == 1:
            here = xc.at[shard(d), j]
            arrived("left", 2 * (d - 1) + j, here)
            if d < 3 or (d == 3 and j == 1):
                send("left", 2 * d + j, here, here, left)
            send("pair", 2 * d + j, here, here, sibling)

    tiles_on(1)
    for d in range(1, 4):
        acts_in(d, 0)
        acts_in(d, 1)
        tiles_in(d)
    tiles_in(4)
    acts_in(4, 0)
    acts_in(4, 1)
    for dy in range(NY):
        for j in range(2):
            arrived("pair", 2 * dy + j, xc.at[shard(dy, True), j])

    table = mall[:, 0, :]
    mv[...] = table
    rows = lax.broadcasted_iota(jnp.int32, (32, 128), 0)
    lanes = lax.broadcasted_iota(jnp.int32, (32, 128), 1)
    derived = jnp.zeros((32, 128), jnp.int32)
    for matrix, first in ((0, 2), (1, 6)):
        cols = [
            jnp.sum(jnp.where(lanes == first + k, table, 0), axis=1, keepdims=True) for k in range(2)
        ]
        flat = jnp.sum(
            jnp.where(rows == lanes // 2, jnp.where(lanes % 2 == 0, cols[0], cols[1]), 0),
            axis=0, keepdims=True,
        )
        for k in range(2):
            same = (flat == cols[k]) & (lanes < 2 * rows + k)
            before = jnp.max(jnp.where(same, lanes + 1, 0), axis=1, keepdims=True)
            derived = jnp.where(lanes == 2 * matrix + k, before, derived)
        ends = jnp.max(jnp.where((flat == rows) & (lanes < 64), lanes + 1, 0), axis=1, keepdims=True)
        derived = jnp.where(lanes == 4 + matrix, ends, derived)
    dv[...] = derived
    copies = [
        pltpu.make_async_copy(mv, ms, local_sems.at[0]),
        pltpu.make_async_copy(dv, md, local_sems.at[1]),
    ]
    for copy in copies:
        copy.start()
    for copy in copies:
        copy.wait()

    lane = lax.broadcasted_iota(jnp.int32, (1, 128), 1)
    low = lane < BLK
    high = jnp.where(low, 0, 1)

    def places(c, first):
        found = []
        for i in range(2):
            for k in range(2):
                place = ms[2 * c + i, first + k] + 3 * i
                found.append([(high + 2 * t) == place for t in range(3)])
        return found

    def forward(c, carry):
        ones, twos = places(c, 0), places(c, 4)
        for i in range(2):
            pack = wall[c // 2, (c % 2) * 2 + i].astype(F32)
            turned = pltpu.roll(pack, BLK, 1)
            first = jnp.where(low, pack, turned)
            second = jnp.where(low, turned, pack)
            for k in range(2):
                n = 2 * i + k
                for t in range(3):
                    span = pl.ds(128 * t, 128)
                    a1[c, pl.ds(BLK * n, BLK), span] = jnp.where(
                        ones[n][t], first[BLK * k : BLK * (k + 1)], 0.0
                    ).astype(BF16)
                    a2[pl.ds(BLK * n, BLK), span] = jnp.where(
                        twos[n][t], second[BLK * k : BLK * (k + 1)], 0.0
                    ).astype(BF16)
        pre = lax.dot_general(a1[c], xc[c, 0], NT, preferred_element_type=F32)
        back = lax.dot_general(a2[...], xc[c, 1], NT, preferred_element_type=F32)
        for n in range(4):
            k = n % 2
            r = 2 * c + n // 2
            hid[1 + 4 * c + n] = pre[BLK * n : BLK * (n + 1)] + hid[md[r, k]]
            ups[1 + 4 * c + n] = back[BLK * n : BLK * (n + 1)] + ups[md[r, 2 + k]]
        return carry

    lax.fori_loop(0, 16, forward, 0)

    def middle(q, carry):
        gelu_out, gelu_slope = gelu_pair(hid[md[q, 4]])
        act[q] = gelu_out.astype(BF16)
        grd[q] = (ups[md[q, 5]] * gelu_slope).astype(BF16)
        return carry

    lax.fori_loop(0, 24, middle, 0)

    def pick(product, found):
        total = jnp.where(found[0], product[:, 0:128], 0.0)
        for t in range(1, 3):
            total = total + jnp.where(found[t], product[:, 128 * t : 128 * (t + 1)], 0.0)
        return total + pltpu.roll(total, BLK, 1)

    def backward(c):
        ones, twos = places(c, 0), places(c, 4)
        slots = [(2 * c + n // 2, n % 2) for n in range(4)]
        grads = jnp.concatenate([grd[ms[r, 2 + k]] for r, k in slots], axis=0)
        acts = jnp.concatenate([act[ms[r, 6 + k]] for r, k in slots], axis=0)
        part[c] = lax.dot_general(grads, a1[c], TN, preferred_element_type=F32).astype(BF16)
        one = lax.dot_general(grads, xc[c, 0], NN, preferred_element_type=F32)
        two = lax.dot_general(acts, xc[c, 1], NN, preferred_element_type=F32)
        for n in range(4):
            span = slice(BLK * n, BLK * (n + 1))
            both = jnp.where(low, pick(one[span], ones[n]), pick(two[span], twos[n]))
            gr[c // 2, (c % 2) * 2 + n // 2, pl.ds(BLK * (n % 2), BLK), :] = both.astype(BF16)

    def settle(dy):
        there = (y + dy) % NY
        arrived("part", dy, psib.at[there])
        total = part[shard(dy)].astype(F32) + psib[there].astype(F32)
        if dy == 4:
            ssum[there] = total.astype(BF16)
            send("cr", 0, ssum.at[there, pl.ds(0, 64)], rbr.at[0, pl.ds(0, 64)], right)
            send("cl", 0, ssum.at[there, pl.ds(64, 64)], rbl.at[0, pl.ds(64, 64)], left)
        elif dy == 3:
            arrived("cr", 0, rbr.at[0, pl.ds(0, 64)])
            ssum[there, pl.ds(0, 64)] = (total[:64] + rbr[0, pl.ds(0, 64)].astype(F32)).astype(BF16)
            ssum[there, pl.ds(64, 64)] = total[64:].astype(BF16)
            send("cr", 1, ssum.at[there], rbr.at[1], right)
        elif dy == 5:
            arrived("cl", 0, rbl.at[0, pl.ds(64, 64)])
            ssum[there, pl.ds(0, 64)] = total[:64].astype(BF16)
            ssum[there, pl.ds(64, 64)] = (total[64:] + rbl[0, pl.ds(64, 64)].astype(F32)).astype(BF16)
            send("cl", 1, ssum.at[there], rbl.at[1], left)
        elif dy in (1, 2):
            arrived("cr", 3 - dy, rbr.at[3 - dy])
            ssum[there] = (total + rbr[3 - dy].astype(F32)).astype(BF16)
            send("cr", 4 - dy, ssum.at[there], rbr.at[4 - dy], right)
        elif dy in (6, 7):
            arrived("cl", dy - 5, rbl.at[dy - 5])
            ssum[there] = (total + rbl[dy - 5].astype(F32)).astype(BF16)
            send("cl", dy - 4, ssum.at[there], rbl.at[dy - 4], left)
        else:
            arrived("cr", 3, rbr.at[3])
            arrived("cl", 3, rbl.at[3])
            ig[...] = total + rbr[3].astype(F32) + rbl[3].astype(F32)

    before = None
    for dy in (4, 3, 5, 2, 6, 1, 7, 0):
        there = (y + dy) % NY

        def both_cores(cc, carry, there=there):
            backward(there * 2 + cc)
            return carry

        lax.fori_loop(0, 2, both_cores, 0)
        send("part", dy, part.at[shard(dy, True)], psib.at[there], sibling)
        for e in range(1, NX):
            send("gx", there * 3 + e - 1, gr.at[there, (x + e) % NX], xr.at[there, e - 1], dev(dx=e))
        if before is not None:
            settle(before)
        before = dy

    def plane_sum(there):
        total = gr[there, x].astype(F32)
        for e in range(1, NX):
            arrived("gx", there * 3 + e - 1, xr.at[there, e - 1])
            total = total + xr[there, e - 1].astype(F32)
        return total

    for e in range(1, NZ):
        there = plane(e)
        zs[there] = plane_sum(there).astype(BF16)
        send("gz", e - 1, zs.at[there], zr.at[e - 1], dev(dz=e))
    settle(before)
    total = plane_sum(z)
    for e in range(1, NZ):
        arrived("gz", e - 1, zr.at[e - 1])
        total = total + zr[e - 1].astype(F32)
    wg[...] = total * scale

    for copy in pending:
        copy.wait_send()


def shards(tokens, cotangent, w1_blocks, w1_coords, w1_count, w2_blocks, w2_coords, w2_count):
    one = w1_blocks.reshape(2, BLK, BLK)
    two = w2_blocks.reshape(2, BLK, BLK)
    pack = jnp.concatenate(
        [jnp.swapaxes(one, 1, 2).reshape(2 * BLK, BLK), two.reshape(2 * BLK, BLK)], axis=1
    )
    slot = jnp.arange(2, dtype=jnp.int32)
    c1, c2 = w1_coords.reshape(2, 2), w2_coords.reshape(2, 2)
    facts = jnp.concatenate([
        jnp.where(slot < w1_count.reshape(1), c1[:, 0], DEAD), c1[:, 1],
        jnp.where(slot < w2_count.reshape(1), c2[:, 1], DEAD), c2[:, 0],
    ])
    meta = jnp.broadcast_to(jnp.pad(facts, (0, 120))[None, :], (8, 128))
    scale = 1.0 / math.sqrt(4096)
    shard = (128, 384)
    vmem = pl.BlockSpec(memory_space=pltpu.VMEM)
    input_grad, grads = pl.pallas_call(
        functools.partial(kernel, scale),
        out_shape=(
            jax.ShapeDtypeStruct(shard, F32),
            jax.ShapeDtypeStruct((128, 128), F32),
        ),
        in_specs=[vmem] * 4,
        out_specs=(vmem, vmem),
        scratch_shapes=[
            pltpu.VMEM((16, 2) + shard, BF16),
            pltpu.VMEM((NZ, NX, 128, 128), BF16),
            pltpu.VMEM((32, 8, 128), jnp.int32),
            pltpu.VMEM((16, 256, 384), BF16),
            pltpu.VMEM((256, 384), BF16),
            pltpu.VMEM((65, BLK, 128), F32),
            pltpu.VMEM((65, BLK, 128), F32),
            pltpu.VMEM((24, BLK, 128), BF16),
            pltpu.VMEM((24, BLK, 128), BF16),
            pltpu.VMEM((16,) + shard, BF16),
            pltpu.VMEM((8,) + shard, BF16),
            pltpu.VMEM((8,) + shard, BF16),
            pltpu.VMEM((4,) + shard, BF16),
            pltpu.VMEM((4,) + shard, BF16),
            pltpu.VMEM((NZ, NX, 128, 128), BF16),
            pltpu.VMEM((NZ, 3, 128, 128), BF16),
            pltpu.VMEM((NZ, 128, 128), BF16),
            pltpu.VMEM((7, 128, 128), BF16),
            pltpu.VMEM((32, 128), jnp.int32),
            pltpu.VMEM((32, 128), jnp.int32),
            pltpu.SMEM((32, 128), jnp.int32),
            pltpu.SMEM((32, 128), jnp.int32),
            pltpu.SemaphoreType.DMA((TOTAL,)),
            pltpu.SemaphoreType.DMA((TOTAL,)),
            pltpu.SemaphoreType.DMA((2,)),
        ],
        compiler_params=pltpu.CompilerParams(
            collective_id=0, has_side_effects=True, vmem_limit_bytes=40 * 1024 * 1024
        ),
        cost_estimate=pl.CostEstimate(
            flops=16 * 5 * 2 * 256 * 384 * 128, bytes_accessed=1 << 20, transcendentals=24 * 64 * 128
        ),
    )(tokens, cotangent, pack, meta)
    grad_one = jnp.swapaxes(grads[:, :BLK].reshape(2, BLK, BLK), 1, 2).reshape(w1_blocks.shape)
    grad_two = grads[:, BLK:].reshape(w2_blocks.shape)
    return (input_grad, grad_one, grad_two)


def solution(mesh):
    wide = P("row", "col", None, None, None)
    return jax.shard_map(
        shards,
        mesh=mesh,
        in_specs=(
            P("row", "col"), P("row", "col"),
            wide, P("row", "col", None, None), P("row", "col"),
            wide, P("row", "col", None, None), P("row", "col"),
        ),
        out_specs=(P("row", "col"), wide, wide),
        check_vma=False,
    )
```

```python
import functools
import math

import jax
import jax.numpy as jnp
from jax import lax
from jax.experimental import pallas as pl
from jax.experimental.pallas import tpu as pltpu
from jax.sharding import PartitionSpec as P

MESH = pl.DeviceIdType.MESH
F32 = jnp.float32
BF16 = jnp.bfloat16
NT = (((1,), (1,)), ((), ()))
NN = (((1,), (0,)), ((), ()))
TN = (((0,), (0,)), ((), ()))
NZ, NX, NY = 8, 4, 8
BLK = 64
DEAD = -64

FAMILIES = (
    ("right", 16), ("left", 16), ("pair", 16),
    ("table_z", 8), ("tile_z", 8), ("table_x", 24), ("tile_x", 24),
    ("part", 8), ("cr", 16), ("cl", 16), ("gx", 24), ("gz", 8),
)
BASE = {}
TOTAL = 0
for family, amount in FAMILIES:
    BASE[family] = TOTAL
    TOTAL += amount


def gelu_pair(hidden):
    inner = 0.7978845608028654 * (hidden + 0.044715 * hidden * hidden * hidden)
    tanh_term = jnp.tanh(inner)
    gelu_out = 0.5 * hidden * (1.0 + tanh_term)
    gelu_slope = 0.5 * (1.0 + tanh_term) + 0.5 * hidden * (
        1.0 - tanh_term * tanh_term
    ) * 0.7978845608028654 * (1.0 + 3.0 * 0.044715 * hidden * hidden)
    return (gelu_out, gelu_slope)


def place_in_order(row, y, core):
    dy = (row // 4 - y + NY) % NY
    other = jnp.where((row // 2) % 2 == core, 0, 1)
    near = jnp.minimum(dy, NY - dy)
    inner = 4 * near - 2 + 2 * other + jnp.where(dy > 4, 1, 0)
    return jnp.where(dy == 0, other, jnp.where(dy == 4, 14 + other, inner))


def kernel(
    tok, cot, w1, w2, coord1, count1, coord2, count2, ig, wg,
    w1v, w2v, c1, n1, c2, n2, xc, wall, mall, a1, a2, hid, ups, act, grd, part, psib, ssum, rbr, rbl,
    gr, xr, zs, zr, mv, dv, ms, md, send_sems, recv_sems, local_sems,
):
    row, col = lax.axis_index("row"), lax.axis_index("col")
    z, x, y, core = row // NX, row % NX, col // 2, col % 2

    def dev(dz=0, dx=0, dy=0, other=False):
        there = (1 - core) if other else core
        return ((z + dz) % NZ * NX + (x + dx) % NX, (y + dy) % NY * 2 + there)

    sibling = dev(other=True)
    right, left = dev(dy=1), dev(dy=NY - 1)
    z_right, z_left = dev(dz=1), dev(dz=NZ - 1)

    barrier = pltpu.get_barrier_semaphore()
    partners = [sibling, right, left]
    partners += [dev(dx=e) for e in range(1, NX)]
    partners += [dev(dz=e) for e in range(1, NZ)]
    for partner in partners:
        pl.semaphore_signal(barrier, inc=1, device_id=partner, device_id_type=MESH)

    loads = [
        pltpu.make_async_copy(src, dst, local_sems.at[n])
        for n, (src, dst) in enumerate((
            (w1, w1v), (w2, w2v), (coord1, c1), (count1, n1), (coord2, c2), (count2, n2),
            (tok, xc.at[col, 0]), (cot, xc.at[col, 1]),
        ))
    ]
    for load in loads:
        load.start()

    pending = []

    def describe(family, n, src, dst, target):
        slot = BASE[family] + n
        return pltpu.make_async_remote_copy(
            src_ref=src, dst_ref=dst, send_sem=send_sems.at[slot], recv_sem=recv_sems.at[slot],
            device_id=target, device_id_type=MESH,
        )

    def send(family, n, src, dst, target):
        copy = describe(family, n, src, dst, target)
        copy.start()
        pending.append(copy)

    def arrived(family, n, dst):
        describe(family, n, dst, dst, sibling).wait_recv()

    def shard(dy, other=False):
        return (y + dy) % NY * 2 + ((1 - core) if other else core)

    def plane(dz):
        return (z + dz) % NZ

    def piece(ref, j, h):
        return ref.at[j, pl.ds(64 * h, 64)]

    pl.semaphore_wait(barrier, len(partners))
    for j, own in ((0, tok), (1, cot)):
        for h in range(2):
            there = piece(xc.at[col], j, h)
            send("right", 2 * j + h, own.at[pl.ds(64 * h, 64)], there, right)
            send("left", 2 * j + h, own.at[pl.ds(64 * h, 64)], there, left)

    lane = lax.broadcasted_iota(jnp.int32, (1, 128), 1)
    low = lane < BLK
    for load in loads[:6]:
        load.wait()
    for k in range(2):
        wall[z, x, pl.ds(BLK * k, BLK), :] = jnp.concatenate(
            [w1v[k].astype(F32).T, w2v[k].astype(F32)], axis=1
        ).astype(BF16)
    hidden_places = [c1[0, 1], c1[1, 1], c2[0, 0], c2[1, 0]]
    model_places = [
        jnp.where(0 < n1[0, 0], c1[0, 0], DEAD), jnp.where(1 < n1[0, 0], c1[1, 0], DEAD),
        jnp.where(0 < n2[0, 0], c2[0, 1], DEAD), jnp.where(1 < n2[0, 0], c2[1, 1], DEAD),
    ]
    lane8 = lax.broadcasted_iota(jnp.int32, (8, 128), 1)
    line8 = lax.broadcasted_iota(jnp.int32, (8, 128), 0)
    meta = jnp.zeros((8, 128), jnp.int32)
    for n in range(4):
        meta = jnp.where((line8 == 0) & (lane8 == n), hidden_places[n], meta)
        meta = jnp.where(line8 == 1 + n, model_places[n], meta)
    mall[row] = meta

    def along_x(dz):
        there = plane(dz)
        for e in range(1, NX):
            at = mall.at[there * NX + x]
            send("table_x", 3 * dz + e - 1, at, at, dev(dx=e))
        for e in range(1, NX):
            at = wall.at[there, x]
            send("tile_x", 3 * dz + e - 1, at, at, dev(dx=e))

    for e in (1, 7, 2, 6, 3, 5, 4):
        send("table_z", e, mall.at[row], mall.at[row], dev(dz=e))
        send("tile_z", e, wall.at[z, x], wall.at[z, x], dev(dz=e))
    along_x(0)

    def planes_in(*away):
        for dz in away:
            arrived("table_z", NZ - dz, mall.at[plane(dz) * NX + x])
            arrived("tile_z", NZ - dz, wall.at[plane(dz), x])
            along_x(dz)

    def tables_in(*away):
        for dz in away:
            for e in range(1, NX):
                arrived("table_x", 3 * dz + e - 1, mall.at[plane(dz) * NX + (x + NX - e) % NX])

    def tiles_in(*away):
        for dz in away:
            for e in range(1, NX):
                arrived("tile_x", 3 * dz + e - 1, wall.at[plane(dz), (x + NX - e) % NX])

    hid[0] = jnp.zeros((BLK, 128), F32)
    ups[0] = jnp.zeros((BLK, 128), F32)
    for load in loads[6:]:
        load.wait()
    for j, own in ((0, tok), (1, cot)):
        send("pair", j, own, xc.at[col, j], sibling)

    def acts_in(d, j, h):
        n = 4 * (d - 1) + 2 * j + h
        if d <= 3 or j == 0:
            back = piece(xc.at[shard(NY - d)], j, h)
            arrived("right", n, back)
            if d < 3 or (d == 3 and j == 0):
                send("right", n + 4, back, back, right)
        if d <= 3 or j == 1:
            ahead = piece(xc.at[shard(d)], j, h)
            arrived("left", n, ahead)
            if d < 3 or (d == 3 and j == 1):
                send("left", n + 4, ahead, ahead, left)
        if h == 1:
            if d <= 3 or j == 0:
                whole = xc.at[shard(NY - d), j]
                send("pair", 2 * (NY - d) + j, whole, whole, sibling)
            if d <= 3 or j == 1:
                whole = xc.at[shard(d), j]
                send("pair", 2 * d + j, whole, whole, sibling)

    def places(c, matrix):
        found = []
        for i in range(2):
            for k in range(2):
                place = mall[2 * c + i, pl.ds(1 + 2 * matrix + k, 1), :] + 3 * i
                found.append([(jnp.where(low, 0, 1) + 2 * t) == place for t in range(3)])
        return found

    def build(c):
        ones, twos = places(c, 0), places(c, 1)
        for i in range(2):
            pack = wall[c // 2, (c % 2) * 2 + i].astype(F32)
            turned = pltpu.roll(pack, BLK, 1)
            first = jnp.where(low, pack, turned)
            second = jnp.where(low, turned, pack)
            for k in range(2):
                n = 2 * i + k
                here = slice(BLK * k, BLK * (k + 1))
                for t in range(3):
                    span = pl.ds(128 * t, 128)
                    a1[c, pl.ds(BLK * n, BLK), span] = jnp.where(ones[n][t], first[here], 0.0).astype(BF16)
                    a2[c, pl.ds(BLK * n, BLK), span] = jnp.where(twos[n][t], second[here], 0.0).astype(BF16)

    def build_planes(*away):
        for dz in away:
            there = plane(dz)

            def one_core(cc, carry, there=there):
                build(2 * there + cc)
                return carry

            lax.fori_loop(0, 2, one_core, 0)

    weights, sums = (a1, a2), (hid, ups)

    def forward_near(d, arrays, others):
        todo = []
        for other in others:
            for s, dy in enumerate(sorted({d, (NY - d) % NY})):
                place = {0: other, 4: 14 + other}.get(d, 4 * d - 2 + 2 * other + s)
                for j in arrays:
                    if other:
                        arrived("pair", 2 * dy + j, xc.at[shard(dy, True), j])
                    todo.append((j, shard(dy, other), place))
        for j, c, place in todo:
            product = lax.dot_general(weights[j][c], xc[c, j], NT, preferred_element_type=F32)
            sums[j][pl.ds(1 + 4 * place, 4)] = product.reshape(4, BLK, 128)
        for j, c, place in todo:
            for n in range(4):
                earlier = md[2 * c + n // 2, 2 * j + n % 2]
                at = 1 + 4 * place + n
                sums[j][at] = sums[j][at] + sums[j][earlier]

    def sort_slots():
        table = mall[:, 0, :]
        mv[...] = table
        rows = lax.broadcasted_iota(jnp.int32, (32, 128), 0)
        lanes = lax.broadcasted_iota(jnp.int32, (32, 128), 1)
        by_lane = 4 * place_in_order(lanes // 2, y, core) + lanes % 4
        by_row = 4 * place_in_order(rows, y, core) + 2 * (rows % 2)
        derived = jnp.zeros((32, 128), jnp.int32)
        for matrix, first in ((0, 0), (1, 2)):
            cols = [
                jnp.sum(jnp.where(lanes == first + k, table, 0), axis=1, keepdims=True) for k in range(2)
            ]
            flat = jnp.sum(
                jnp.where(rows == lanes // 2, jnp.where(lanes % 2 == 0, cols[0], cols[1]), 0),
                axis=0, keepdims=True,
            )
            for k in range(2):
                same = (flat == cols[k]) & (by_lane < by_row + k) & (lanes < 64)
                before = jnp.max(jnp.where(same, by_lane + 1, 0), axis=1, keepdims=True)
                derived = jnp.where(lanes == 2 * matrix + k, before, derived)
            ends = jnp.max(
                jnp.where((flat == rows) & (lanes < 64), by_lane + 1, 0), axis=1, keepdims=True
            )
            derived = jnp.where(lanes == 4 + matrix, ends, derived)
        dv[...] = derived
        copies = [
            pltpu.make_async_copy(mv, ms, local_sems.at[0]),
            pltpu.make_async_copy(dv, md, local_sems.at[1]),
        ]
        for copy in copies:
            copy.start()
        for copy in copies:
            copy.wait()

    planes_in(1, 7)
    acts_in(1, 0, 0)
    acts_in(1, 0, 1)
    planes_in(2, 6)
    acts_in(1, 1, 0)
    acts_in(1, 1, 1)
    planes_in(3, 5, 4)
    acts_in(2, 0, 0)
    tables_in(0, 1, 7)
    tiles_in(0, 1, 7)
    build_planes(0, 1, 7)
    acts_in(2, 0, 1)
    acts_in(2, 1, 0)
    tables_in(2, 6)
    tiles_in(2, 6)
    build_planes(2, 6)
    acts_in(2, 1, 1)
    tables_in(3, 5, 4)
    sort_slots()
    acts_in(3, 0, 0)
    tiles_in(3, 5, 4)
    build_planes(3, 5, 4)
    acts_in(3, 0, 1)
    forward_near(0, (0, 1), (0, 1))
    forward_near(1, (0,), (0, 1))
    acts_in(3, 1, 0)
    forward_near(1, (1,), (0, 1))
    acts_in(3, 1, 1)
    forward_near(2, (0,), (0, 1))
    forward_near(2, (1,), (0, 1))
    acts_in(4, 0, 0)
    acts_in(4, 1, 0)
    forward_near(3, (0,), (0, 1))
    acts_in(4, 0, 1)
    acts_in(4, 1, 1)
    forward_near(3, (1,), (0, 1))
    forward_near(4, (0, 1), (0,))
    forward_near(4, (0, 1), (1,))

    def middle(q, carry):
        gelu_out, gelu_slope = gelu_pair(hid[md[q, 4]])
        act[q] = gelu_out.astype(BF16)
        grd[q] = (ups[md[q, 5]] * gelu_slope).astype(BF16)
        return carry

    lax.fori_loop(0, 24, middle, 0)

    def pick(product, found):
        total = jnp.where(found[0], product[:, 0:128], 0.0)
        for t in range(1, 3):
            total = total + jnp.where(found[t], product[:, 128 * t : 128 * (t + 1)], 0.0)
        return total + pltpu.roll(total, BLK, 1)

    def chosen(source, c, first):
        return jnp.concatenate([source[ms[2 * c + n // 2, first + n % 2]] for n in range(4)], axis=0)

    def to_input(c):
        part[c] = lax.dot_general(
            chosen(grd, c, 0), a1[c], TN, preferred_element_type=F32
        ).astype(BF16)

    def to_blocks(c):
        ones, twos = places(c, 0), places(c, 1)
        one = lax.dot_general(chosen(grd, c, 0), xc[c, 0], NN, preferred_element_type=F32)
        two = lax.dot_general(chosen(act, c, 2), xc[c, 1], NN, preferred_element_type=F32)
        for n in range(4):
            span = slice(BLK * n, BLK * (n + 1))
            both = jnp.where(low, pick(one[span], ones[n]), pick(two[span], twos[n]))
            gr[c // 2, (c % 2) * 2 + n // 2, pl.ds(BLK * (n % 2), BLK), :] = both.astype(BF16)

    def quarter(ref, q):
        return ref.at[pl.ds(32 * q, 32)]

    def settle(dy, *quarters):
        there = (y + dy) % NY
        for q in quarters:
            rows = pl.ds(32 * q, 32)
            total = part[shard(dy), rows].astype(F32) + psib[there, rows].astype(F32)
            if dy == 0:
                for family, buffer in (("cr", rbr), ("cl", rbl)):
                    arrived(family, 12 + q, quarter(buffer.at[3], q))
                    total = total + buffer[3, rows].astype(F32)
                ig[rows, :] = total
                continue
            chain, step = (0, 4 - dy) if dy < 4 else (1, dy - 4)
            if dy == 4:
                chain = q // 2
            family, buffer, target = (("cr", rbr, right), ("cl", rbl, left))[chain]
            if step > 1 or (step == 1 and q // 2 == chain):
                arrived(family, 4 * step - 4 + q, quarter(buffer.at[step - 1], q))
                total = total + buffer[step - 1, rows].astype(F32)
            ssum[there, rows] = total.astype(BF16)
            send(family, 4 * step + q, quarter(ssum.at[there], q), quarter(buffer.at[step], q), target)

    def paired(*away):
        for dy in away:
            arrived("part", dy, psib.at[(y + dy) % NY])

    def plane_sum(dz):
        total = gr[plane(dz), x].astype(F32)
        for e in range(1, NX):
            arrived("gx", dz * 3 + e - 1, xr.at[dz, e - 1])
            total = total + xr[dz, e - 1].astype(F32)
        return total

    def plane_on(*away):
        for dz in away:
            zs[dz] = plane_sum(dz).astype(BF16)
            send("gz", dz, zs.at[dz], zr.at[dz], dev(dz=dz))

    def inputs_step(dy):
        there = (y + dy) % NY
        for other in (True, False):
            to_input(shard(dy, other))
            if other:
                send("part", dy, part.at[shard(dy, True)], psib.at[there], sibling)

    def blocks_step(dz):
        there = plane(dz)
        for cc in range(2):
            to_blocks(there * 2 + cc)
        for e in range(1, NX):
            send("gx", dz * 3 + e - 1, gr.at[there, (x + e) % NX], xr.at[dz, e - 1], dev(dx=e))

    inputs_step(4)
    inputs_step(3)
    inputs_step(5)
    blocks_step(4)
    paired(4)
    settle(4, 0, 2, 1, 3)
    paired(3, 5)
    settle(3, 2, 3)
    settle(5, 0, 1)
    inputs_step(2)
    blocks_step(3)
    inputs_step(6)
    blocks_step(5)
    for n in range(2):
        settle(3, n)
        settle(5, 2 + n)
    paired(2, 6)
    for n in range(2):
        settle(2, 2 + n)
        settle(6, n)
    inputs_step(1)
    blocks_step(2)
    plane_on(4)
    for n in range(2):
        settle(2, n)
        settle(6, 2 + n)
    inputs_step(7)
    blocks_step(6)
    plane_on(3)
    paired(1, 7)
    for n in range(2):
        settle(1, 2 + n)
        settle(7, n)
    inputs_step(0)
    blocks_step(1)
    plane_on(5)
    for n in range(2):
        settle(1, n)
        settle(7, 2 + n)
    blocks_step(7)
    plane_on(2)
    blocks_step(0)
    plane_on(6)
    paired(0)
    plane_on(1, 7)
    settle(0, 2, 3, 0, 1)
    total = plane_sum(0)
    for e in range(1, NZ):
        arrived("gz", e, zr.at[e])
        total = total + zr[e].astype(F32)
    wg[...] = total

    for copy in pending:
        copy.wait_send()


def finish(scale, ig, wg, input_grad, grad_one, grad_two, one, two, sems):
    copies = [pltpu.make_async_copy(ig, input_grad, sems.at[0])]
    copies[0].start()
    for k in range(2):
        rows = pl.ds(BLK * k, BLK)
        one[k] = wg[rows, 0:BLK].T * scale
        two[k] = wg[rows, BLK : 2 * BLK] * scale
    copies.append(pltpu.make_async_copy(one, grad_one, sems.at[1]))
    copies.append(pltpu.make_async_copy(two, grad_two, sems.at[2]))
    for copy in copies[1:]:
        copy.start()
    for copy in copies:
        copy.wait()


def shards(tokens, cotangent, w1_blocks, w1_coords, w1_count, w2_blocks, w2_coords, w2_count):
    scale = 1.0 / math.sqrt(4096)
    shard = (128, 384)
    blocks = (2, BLK, BLK)
    vmem = pl.BlockSpec(memory_space=pltpu.VMEM)
    anywhere = pl.BlockSpec(memory_space=pl.ANY)
    ig, wg = pl.pallas_call(
        kernel,
        out_shape=(
            jax.ShapeDtypeStruct(shard, F32),
            jax.ShapeDtypeStruct((128, 128), F32),
        ),
        in_specs=[anywhere] * 8,
        out_specs=(vmem, vmem),
        scratch_shapes=[
            pltpu.VMEM(blocks, BF16),
            pltpu.VMEM(blocks, BF16),
            pltpu.SMEM((2, 2), jnp.int32),
            pltpu.SMEM((1, 1), jnp.int32),
            pltpu.SMEM((2, 2), jnp.int32),
            pltpu.SMEM((1, 1), jnp.int32),
            pltpu.VMEM((16, 2) + shard, BF16),
            pltpu.VMEM((NZ, NX, 128, 128), BF16),
            pltpu.VMEM((32, 8, 128), jnp.int32),
            pltpu.VMEM((16, 256, 384), BF16),
            pltpu.VMEM((16, 256, 384), BF16),
            pltpu.VMEM((65, BLK, 128), F32),
            pltpu.VMEM((65, BLK, 128), F32),
            pltpu.VMEM((24, BLK, 128), BF16),
            pltpu.VMEM((24, BLK, 128), BF16),
            pltpu.VMEM((16,) + shard, BF16),
            pltpu.VMEM((8,) + shard, BF16),
            pltpu.VMEM((8,) + shard, BF16),
            pltpu.VMEM((4,) + shard, BF16),
            pltpu.VMEM((4,) + shard, BF16),
            pltpu.VMEM((NZ, NX, 128, 128), BF16),
            pltpu.VMEM((NZ, 3, 128, 128), BF16),
            pltpu.VMEM((NZ, 128, 128), BF16),
            pltpu.VMEM((NZ, 128, 128), BF16),
            pltpu.VMEM((32, 128), jnp.int32),
            pltpu.VMEM((32, 128), jnp.int32),
            pltpu.SMEM((32, 128), jnp.int32),
            pltpu.SMEM((32, 128), jnp.int32),
            pltpu.SemaphoreType.DMA((TOTAL,)),
            pltpu.SemaphoreType.DMA((TOTAL,)),
            pltpu.SemaphoreType.DMA((8,)),
        ],
        compiler_params=pltpu.CompilerParams(
            collective_id=0, has_side_effects=True, vmem_limit_bytes=56 * 1024 * 1024
        ),
        cost_estimate=pl.CostEstimate(
            flops=16 * 5 * 2 * 256 * 384 * 128, bytes_accessed=1 << 20, transcendentals=24 * 64 * 128
        ),
    )(
        tokens, cotangent, w1_blocks.reshape(blocks), w2_blocks.reshape(blocks),
        w1_coords.reshape(2, 2), w1_count, w2_coords.reshape(2, 2), w2_count,
    )
    input_grad, grad_one, grad_two = pl.pallas_call(
        functools.partial(finish, scale),
        out_shape=(
            jax.ShapeDtypeStruct(shard, F32),
            jax.ShapeDtypeStruct(blocks, F32),
            jax.ShapeDtypeStruct(blocks, F32),
        ),
        in_specs=[vmem] * 2,
        out_specs=(anywhere,) * 3,
        scratch_shapes=[
            pltpu.VMEM(blocks, F32), pltpu.VMEM(blocks, F32), pltpu.SemaphoreType.DMA((3,)),
        ],
    )(ig, wg)
    return (input_grad, grad_one.reshape(w1_blocks.shape), grad_two.reshape(w2_blocks.shape))


def solution(mesh):
    wide = P("row", "col", None, None, None)
    return jax.shard_map(
        shards,
        mesh=mesh,
        in_specs=(
            P("row", "col"), P("row", "col"),
            wide, P("row", "col", None, None), P("row", "col"),
            wide, P("row", "col", None, None), P("row", "col"),
        ),
        out_specs=(P("row", "col"), wide, wide),
        check_vma=False,
    )
```

```python
import functools
import math

import jax
import jax.numpy as jnp
from jax import lax
from jax.experimental import pallas as pl
from jax.experimental.pallas import tpu as pltpu
from jax.sharding import PartitionSpec as P

MESH = pl.DeviceIdType.MESH
F32 = jnp.float32
BF16 = jnp.bfloat16
NT = (((1,), (1,)), ((), ()))
NN = (((1,), (0,)), ((), ()))
TN = (((0,), (0,)), ((), ()))
NZ, NX, NY = 8, 4, 8
BLK = 64
DEAD = -64

FAMILIES = (
    ("right", 16), ("left", 16), ("pair", 16),
    ("table_z", 8), ("tile_z", 8), ("table_x", 24), ("tile_x", 24),
    ("part", 8), ("cr", 16), ("cl", 16), ("gx", 24), ("gz", 8),
)
BASE = {}
TOTAL = 0
for family, amount in FAMILIES:
    BASE[family] = TOTAL
    TOTAL += amount


def gelu_pair(hidden):
    inner = 0.7978845608028654 * (hidden + 0.044715 * hidden * hidden * hidden)
    tanh_term = jnp.tanh(inner)
    gelu_out = 0.5 * hidden * (1.0 + tanh_term)
    gelu_slope = 0.5 * (1.0 + tanh_term) + 0.5 * hidden * (
        1.0 - tanh_term * tanh_term
    ) * 0.7978845608028654 * (1.0 + 3.0 * 0.044715 * hidden * hidden)
    return (gelu_out, gelu_slope)


def place_in_order(row, y, core):
    dy = (row // 4 - y + NY) % NY
    other = jnp.where((row // 2) % 2 == core, 0, 1)
    near = jnp.minimum(dy, NY - dy)
    inner = 4 * near - 2 + 2 * other + jnp.where(dy > 4, 1, 0)
    return jnp.where(dy == 0, other, jnp.where(dy == 4, 14 + other, inner))


def kernel(
    scale, tok, cot, w1, w2, coord1, count1, coord2, count2, ig, g1, g2,
    w1v, w2v, c1, n1, c2, n2, xc, wall, mall, a1, a2, hid, ups, act, grd, part, psib, ssum, rbr, rbl,
    igv, g1v, g2v, gr, xr, zs, zr, mv, dv, ms, md, send_sems, recv_sems, local_sems,
):
    row, col = lax.axis_index("row"), lax.axis_index("col")
    z, x, y, core = row // NX, row % NX, col // 2, col % 2

    def dev(dz=0, dx=0, dy=0, other=False):
        there = (1 - core) if other else core
        return ((z + dz) % NZ * NX + (x + dx) % NX, (y + dy) % NY * 2 + there)

    sibling = dev(other=True)
    right, left = dev(dy=1), dev(dy=NY - 1)
    z_right, z_left = dev(dz=1), dev(dz=NZ - 1)

    barrier = pltpu.get_barrier_semaphore()
    partners = [sibling, right, left]
    partners += [dev(dx=e) for e in range(1, NX)]
    partners += [dev(dz=e) for e in range(1, NZ)]
    for partner in partners:
        pl.semaphore_signal(barrier, inc=1, device_id=partner, device_id_type=MESH)

    loads = [
        pltpu.make_async_copy(src, dst, local_sems.at[n])
        for n, (src, dst) in enumerate((
            (w1, w1v), (w2, w2v), (coord1, c1), (count1, n1), (coord2, c2), (count2, n2),
            (tok, xc.at[col, 0]), (cot, xc.at[col, 1]),
        ))
    ]
    for load in loads:
        load.start()

    pending = []

    def describe(family, n, src, dst, target):
        slot = BASE[family] + n
        return pltpu.make_async_remote_copy(
            src_ref=src, dst_ref=dst, send_sem=send_sems.at[slot], recv_sem=recv_sems.at[slot],
            device_id=target, device_id_type=MESH,
        )

    def send(family, n, src, dst, target):
        copy = describe(family, n, src, dst, target)
        copy.start()
        pending.append(copy)

    def arrived(family, n, dst):
        describe(family, n, dst, dst, sibling).wait_recv()

    def shard(dy, other=False):
        return (y + dy) % NY * 2 + ((1 - core) if other else core)

    def plane(dz):
        return (z + dz) % NZ

    def piece(ref, j, h):
        return ref.at[j, pl.ds(64 * h, 64)]

    pl.semaphore_wait(barrier, len(partners))
    for j, own in ((0, tok), (1, cot)):
        for h in range(2):
            there = piece(xc.at[col], j, h)
            send("right", 2 * j + h, own.at[pl.ds(64 * h, 64)], there, right)
            send("left", 2 * j + h, own.at[pl.ds(64 * h, 64)], there, left)

    lane = lax.broadcasted_iota(jnp.int32, (1, 128), 1)
    low = lane < BLK
    for load in loads[:6]:
        load.wait()
    for k in range(2):
        wall[z, x, pl.ds(BLK * k, BLK), :] = jnp.concatenate(
            [w1v[k].astype(F32).T, w2v[k].astype(F32)], axis=1
        ).astype(BF16)
    hidden_places = [c1[0, 1], c1[1, 1], c2[0, 0], c2[1, 0]]
    model_places = [
        jnp.where(0 < n1[0, 0], c1[0, 0], DEAD), jnp.where(1 < n1[0, 0], c1[1, 0], DEAD),
        jnp.where(0 < n2[0, 0], c2[0, 1], DEAD), jnp.where(1 < n2[0, 0], c2[1, 1], DEAD),
    ]
    lane8 = lax.broadcasted_iota(jnp.int32, (8, 128), 1)
    line8 = lax.broadcasted_iota(jnp.int32, (8, 128), 0)
    meta = jnp.zeros((8, 128), jnp.int32)
    for n in range(4):
        meta = jnp.where((line8 == 0) & (lane8 == n), hidden_places[n], meta)
        meta = jnp.where(line8 == 1 + n, model_places[n], meta)
    mall[row] = meta

    def along_x(dz):
        there = plane(dz)
        for e in range(1, NX):
            at = mall.at[there * NX + x]
            send("table_x", 3 * dz + e - 1, at, at, dev(dx=e))
        for e in range(1, NX):
            at = wall.at[there, x]
            send("tile_x", 3 * dz + e - 1, at, at, dev(dx=e))

    for e in (1, 7, 2, 6, 3, 5, 4):
        send("table_z", e, mall.at[row], mall.at[row], dev(dz=e))
        send("tile_z", e, wall.at[z, x], wall.at[z, x], dev(dz=e))
    along_x(0)

    def planes_in(*away):
        for dz in away:
            arrived("table_z", NZ - dz, mall.at[plane(dz) * NX + x])
            arrived("tile_z", NZ - dz, wall.at[plane(dz), x])
            along_x(dz)

    def tables_in(*away):
        for dz in away:
            for e in range(1, NX):
                arrived("table_x", 3 * dz + e - 1, mall.at[plane(dz) * NX + (x + NX - e) % NX])

    def tiles_in(*away):
        for dz in away:
            for e in range(1, NX):
                arrived("tile_x", 3 * dz + e - 1, wall.at[plane(dz), (x + NX - e) % NX])

    hid[0] = jnp.zeros((BLK, 128), F32)
    ups[0] = jnp.zeros((BLK, 128), F32)
    for load in loads[6:]:
        load.wait()
    for j, own in ((0, tok), (1, cot)):
        send("pair", j, own, xc.at[col, j], sibling)

    def acts_in(d, j, h):
        n = 4 * (d - 1) + 2 * j + h
        if d <= 3 or j == 0:
            back = piece(xc.at[shard(NY - d)], j, h)
            arrived("right", n, back)
            if d < 3 or (d == 3 and j == 0):
                send("right", n + 4, back, back, right)
        if d <= 3 or j == 1:
            ahead = piece(xc.at[shard(d)], j, h)
            arrived("left", n, ahead)
            if d < 3 or (d == 3 and j == 1):
                send("left", n + 4, ahead, ahead, left)
        if h == 1:
            if d <= 3 or j == 0:
                whole = xc.at[shard(NY - d), j]
                send("pair", 2 * (NY - d) + j, whole, whole, sibling)
            if d <= 3 or j == 1:
                whole = xc.at[shard(d), j]
                send("pair", 2 * d + j, whole, whole, sibling)

    def places(c, matrix):
        found = []
        for i in range(2):
            for k in range(2):
                place = mall[2 * c + i, pl.ds(1 + 2 * matrix + k, 1), :] + 3 * i
                found.append([(jnp.where(low, 0, 1) + 2 * t) == place for t in range(3)])
        return found

    def build(c):
        ones, twos = places(c, 0), places(c, 1)
        for i in range(2):
            pack = wall[c // 2, (c % 2) * 2 + i].astype(F32)
            turned = pltpu.roll(pack, BLK, 1)
            first = jnp.where(low, pack, turned)
            second = jnp.where(low, turned, pack)
            for k in range(2):
                n = 2 * i + k
                here = slice(BLK * k, BLK * (k + 1))
                for t in range(3):
                    span = pl.ds(128 * t, 128)
                    a1[c, pl.ds(BLK * n, BLK), span] = jnp.where(ones[n][t], first[here], 0.0).astype(BF16)
                    a2[c, pl.ds(BLK * n, BLK), span] = jnp.where(twos[n][t], second[here], 0.0).astype(BF16)

    def build_planes(*away):
        for dz in away:
            there = plane(dz)

            def one_core(cc, carry, there=there):
                build(2 * there + cc)
                return carry

            lax.fori_loop(0, 2, one_core, 0)

    weights, sums = (a1, a2), (hid, ups)

    def forward_near(d, arrays, others):
        todo = []
        for other in others:
            for s, dy in enumerate(sorted({d, (NY - d) % NY})):
                place = {0: other, 4: 14 + other}.get(d, 4 * d - 2 + 2 * other + s)
                for j in arrays:
                    if other:
                        arrived("pair", 2 * dy + j, xc.at[shard(dy, True), j])
                    todo.append((j, shard(dy, other), place))
        for j, c, place in todo:
            product = lax.dot_general(weights[j][c], xc[c, j], NT, preferred_element_type=F32)
            sums[j][pl.ds(1 + 4 * place, 4)] = product.reshape(4, BLK, 128)
        for j, c, place in todo:
            for n in range(4):
                earlier = md[2 * c + n // 2, 2 * j + n % 2]
                at = 1 + 4 * place + n
                sums[j][at] = sums[j][at] + sums[j][earlier]

    def sort_slots():
        table = mall[:, 0, :]
        mv[...] = table
        rows = lax.broadcasted_iota(jnp.int32, (32, 128), 0)
        lanes = lax.broadcasted_iota(jnp.int32, (32, 128), 1)
        by_lane = 4 * place_in_order(lanes // 2, y, core) + lanes % 4
        by_row = 4 * place_in_order(rows, y, core) + 2 * (rows % 2)
        derived = jnp.zeros((32, 128), jnp.int32)
        for matrix, first in ((0, 0), (1, 2)):
            cols = [
                jnp.sum(jnp.where(lanes == first + k, table, 0), axis=1, keepdims=True) for k in range(2)
            ]
            flat = jnp.sum(
                jnp.where(rows == lanes // 2, jnp.where(lanes % 2 == 0, cols[0], cols[1]), 0),
                axis=0, keepdims=True,
            )
            for k in range(2):
                same = (flat == cols[k]) & (by_lane < by_row + k) & (lanes < 64)
                before = jnp.max(jnp.where(same, by_lane + 1, 0), axis=1, keepdims=True)
                derived = jnp.where(lanes == 2 * matrix + k, before, derived)
            ends = jnp.max(
                jnp.where((flat == rows) & (lanes < 64), by_lane + 1, 0), axis=1, keepdims=True
            )
            derived = jnp.where(lanes == 4 + matrix, ends, derived)
        dv[...] = derived
        copies = [
            pltpu.make_async_copy(mv, ms, local_sems.at[0]),
            pltpu.make_async_copy(dv, md, local_sems.at[1]),
        ]
        for copy in copies:
            copy.start()
        for copy in copies:
            copy.wait()

    planes_in(1, 7)
    acts_in(1, 0, 0)
    acts_in(1, 0, 1)
    planes_in(2, 6)
    acts_in(1, 1, 0)
    acts_in(1, 1, 1)
    planes_in(3, 5, 4)
    acts_in(2, 0, 0)
    tables_in(0, 1, 7)
    tiles_in(0, 1, 7)
    build_planes(0, 1, 7)
    acts_in(2, 0, 1)
    acts_in(2, 1, 0)
    tables_in(2, 6)
    tiles_in(2, 6)
    build_planes(2, 6)
    acts_in(2, 1, 1)
    tables_in(3, 5, 4)
    sort_slots()
    acts_in(3, 0, 0)
    tiles_in(3, 5, 4)
    build_planes(3, 5, 4)
    acts_in(3, 0, 1)
    forward_near(0, (0, 1), (0, 1))
    forward_near(1, (0,), (0, 1))
    acts_in(3, 1, 0)
    forward_near(1, (1,), (0, 1))
    acts_in(3, 1, 1)
    forward_near(2, (0,), (0, 1))
    forward_near(2, (1,), (0, 1))
    acts_in(4, 0, 0)
    acts_in(4, 1, 0)
    forward_near(3, (0,), (0, 1))
    acts_in(4, 0, 1)
    acts_in(4, 1, 1)
    forward_near(3, (1,), (0, 1))
    forward_near(4, (0, 1), (0,))
    forward_near(4, (0, 1), (1,))

    def middle(q, carry):
        gelu_out, gelu_slope = gelu_pair(hid[md[q, 4]])
        act[q] = gelu_out.astype(BF16)
        grd[q] = (ups[md[q, 5]] * gelu_slope).astype(BF16)
        return carry

    lax.fori_loop(0, 24, middle, 0)

    def pick(product, found):
        total = jnp.where(found[0], product[:, 0:128], 0.0)
        for t in range(1, 3):
            total = total + jnp.where(found[t], product[:, 128 * t : 128 * (t + 1)], 0.0)
        return total + pltpu.roll(total, BLK, 1)

    def chosen(source, c, first):
        return jnp.concatenate([source[ms[2 * c + n // 2, first + n % 2]] for n in range(4)], axis=0)

    def to_input(c):
        part[c] = lax.dot_general(
            chosen(grd, c, 0), a1[c], TN, preferred_element_type=F32
        ).astype(BF16)

    def to_blocks(c):
        ones, twos = places(c, 0), places(c, 1)
        one = lax.dot_general(chosen(grd, c, 0), xc[c, 0], NN, preferred_element_type=F32)
        two = lax.dot_general(chosen(act, c, 2), xc[c, 1], NN, preferred_element_type=F32)
        for n in range(4):
            span = slice(BLK * n, BLK * (n + 1))
            both = jnp.where(low, pick(one[span], ones[n]), pick(two[span], twos[n]))
            gr[c // 2, (c % 2) * 2 + n // 2, pl.ds(BLK * (n % 2), BLK), :] = both.astype(BF16)

    def quarter(ref, q):
        return ref.at[pl.ds(32 * q, 32)]

    def settle(dy, *quarters):
        there = (y + dy) % NY
        for q in quarters:
            rows = pl.ds(32 * q, 32)
            total = part[shard(dy), rows].astype(F32) + psib[there, rows].astype(F32)
            if dy == 0:
                for family, buffer in (("cr", rbr), ("cl", rbl)):
                    arrived(family, 12 + q, quarter(buffer.at[3], q))
                    total = total + buffer[3, rows].astype(F32)
                igv[rows, :] = total
                pltpu.make_async_copy(quarter(igv, q), quarter(ig, q), local_sems.at[q]).start()
                continue
            chain, step = (0, 4 - dy) if dy < 4 else (1, dy - 4)
            if dy == 4:
                chain = q // 2
            family, buffer, target = (("cr", rbr, right), ("cl", rbl, left))[chain]
            if step > 1 or (step == 1 and q // 2 == chain):
                arrived(family, 4 * step - 4 + q, quarter(buffer.at[step - 1], q))
                total = total + buffer[step - 1, rows].astype(F32)
            ssum[there, rows] = total.astype(BF16)
            send(family, 4 * step + q, quarter(ssum.at[there], q), quarter(buffer.at[step], q), target)

    def paired(*away):
        for dy in away:
            arrived("part", dy, psib.at[(y + dy) % NY])

    def plane_sum(dz):
        total = gr[plane(dz), x].astype(F32)
        for e in range(1, NX):
            arrived("gx", dz * 3 + e - 1, xr.at[dz, e - 1])
            total = total + xr[dz, e - 1].astype(F32)
        return total

    def plane_on(*away):
        for dz in away:
            zs[dz] = plane_sum(dz).astype(BF16)
            send("gz", dz, zs.at[dz], zr.at[dz], dev(dz=dz))

    def inputs_step(dy):
        there = (y + dy) % NY
        for other in (True, False):
            to_input(shard(dy, other))
            if other:
                send("part", dy, part.at[shard(dy, True)], psib.at[there], sibling)

    def blocks_step(dz):
        there = plane(dz)
        for cc in range(2):
            to_blocks(there * 2 + cc)
        for e in range(1, NX):
            send("gx", dz * 3 + e - 1, gr.at[there, (x + e) % NX], xr.at[dz, e - 1], dev(dx=e))

    inputs_step(4)
    blocks_step(4)
    inputs_step(3)
    inputs_step(5)
    blocks_step(3)
    blocks_step(5)
    inputs_step(2)
    inputs_step(6)
    paired(4)
    settle(4, 0, 2, 1, 3)
    blocks_step(2)
    paired(3, 5)
    settle(3, 2, 3)
    settle(5, 0, 1)
    blocks_step(6)
    inputs_step(1)
    inputs_step(7)
    blocks_step(1)
    blocks_step(7)
    inputs_step(0)
    blocks_step(0)
    plane_on(4)
    for n in range(2):
        settle(3, n)
        settle(5, 2 + n)
    plane_on(3)
    paired(2, 6)
    for n in range(2):
        settle(2, 2 + n)
        settle(6, n)
    plane_on(5)
    for n in range(2):
        settle(2, n)
        settle(6, 2 + n)
    plane_on(2)
    paired(1, 7)
    for n in range(2):
        settle(1, 2 + n)
        settle(7, n)
    plane_on(6)
    for n in range(2):
        settle(1, n)
        settle(7, 2 + n)
    plane_on(1)
    plane_on(7)
    paired(0)
    settle(0, 2, 3, 0, 1)
    total = plane_sum(0)
    for e in range(1, NZ):
        arrived("gz", e, zr.at[e])
        total = total + zr[e].astype(F32)
    total = total * scale
    for k in range(2):
        here = slice(BLK * k, BLK * (k + 1))
        g1v[k] = total[here, 0:BLK].T
        g2v[k] = total[here, BLK:128]
    stores = [
        pltpu.make_async_copy(g1v, g1, local_sems.at[4]),
        pltpu.make_async_copy(g2v, g2, local_sems.at[5]),
    ]
    for store in stores:
        store.start()
    for q in range(4):
        pltpu.make_async_copy(quarter(igv, q), quarter(ig, q), local_sems.at[q]).wait()
    for store in stores:
        store.wait()

    for copy in pending:
        copy.wait_send()


def finish(ig, g1, g2, input_grad, grad_one, grad_two, sems):
    copies = [
        pltpu.make_async_copy(src, dst, sems.at[n])
        for n, (src, dst) in enumerate(((ig, input_grad), (g1, grad_one), (g2, grad_two)))
    ]
    for copy in copies:
        copy.start()
    for copy in copies:
        copy.wait()


def shards(tokens, cotangent, w1_blocks, w1_coords, w1_count, w2_blocks, w2_coords, w2_count):
    scale = 1.0 / math.sqrt(4096)
    shard = (128, 384)
    blocks = (2, BLK, BLK)
    anywhere = pl.BlockSpec(memory_space=pl.ANY)
    results = (
        jax.ShapeDtypeStruct(shard, F32),
        jax.ShapeDtypeStruct(blocks, F32),
        jax.ShapeDtypeStruct(blocks, F32),
    )
    halfway = pl.pallas_call(
        functools.partial(kernel, scale),
        out_shape=results,
        in_specs=[anywhere] * 8,
        out_specs=(anywhere,) * 3,
        scratch_shapes=[
            pltpu.VMEM(blocks, BF16),
            pltpu.VMEM(blocks, BF16),
            pltpu.SMEM((2, 2), jnp.int32),
            pltpu.SMEM((1, 1), jnp.int32),
            pltpu.SMEM((2, 2), jnp.int32),
            pltpu.SMEM((1, 1), jnp.int32),
            pltpu.VMEM((16, 2) + shard, BF16),
            pltpu.VMEM((NZ, NX, 128, 128), BF16),
            pltpu.VMEM((32, 8, 128), jnp.int32),
            pltpu.VMEM((16, 256, 384), BF16),
            pltpu.VMEM((16, 256, 384), BF16),
            pltpu.VMEM((65, BLK, 128), F32),
            pltpu.VMEM((65, BLK, 128), F32),
            pltpu.VMEM((24, BLK, 128), BF16),
            pltpu.VMEM((24, BLK, 128), BF16),
            pltpu.VMEM((16,) + shard, BF16),
            pltpu.VMEM((8,) + shard, BF16),
            pltpu.VMEM((8,) + shard, BF16),
            pltpu.VMEM((4,) + shard, BF16),
            pltpu.VMEM((4,) + shard, BF16),
            pltpu.VMEM(shard, F32),
            pltpu.VMEM(blocks, F32),
            pltpu.VMEM(blocks, F32),
            pltpu.VMEM((NZ, NX, 128, 128), BF16),
            pltpu.VMEM((NZ, 3, 128, 128), BF16),
            pltpu.VMEM((NZ, 128, 128), BF16),
            pltpu.VMEM((NZ, 128, 128), BF16),
            pltpu.VMEM((32, 128), jnp.int32),
            pltpu.VMEM((32, 128), jnp.int32),
            pltpu.SMEM((32, 128), jnp.int32),
            pltpu.SMEM((32, 128), jnp.int32),
            pltpu.SemaphoreType.DMA((TOTAL,)),
            pltpu.SemaphoreType.DMA((TOTAL,)),
            pltpu.SemaphoreType.DMA((8,)),
        ],
        compiler_params=pltpu.CompilerParams(
            collective_id=0, has_side_effects=True, vmem_limit_bytes=56 * 1024 * 1024
        ),
        cost_estimate=pl.CostEstimate(
            flops=16 * 5 * 2 * 256 * 384 * 128, bytes_accessed=1 << 20, transcendentals=24 * 64 * 128
        ),
    )(
        tokens, cotangent, w1_blocks.reshape(blocks), w2_blocks.reshape(blocks),
        w1_coords.reshape(2, 2), w1_count, w2_coords.reshape(2, 2), w2_count,
    )
    input_grad, grad_one, grad_two = pl.pallas_call(
        finish,
        out_shape=results,
        in_specs=[pl.BlockSpec(memory_space=pltpu.VMEM)] * 3,
        out_specs=(anywhere,) * 3,
        scratch_shapes=[pltpu.SemaphoreType.DMA((3,))],
    )(*halfway)
    return (input_grad, grad_one.reshape(w1_blocks.shape), grad_two.reshape(w2_blocks.shape))


def solution(mesh):
    wide = P("row", "col", None, None, None)
    return jax.shard_map(
        shards,
        mesh=mesh,
        in_specs=(
            P("row", "col"), P("row", "col"),
            wide, P("row", "col", None, None), P("row", "col"),
            wide, P("row", "col", None, None), P("row", "col"),
        ),
        out_specs=(P("row", "col"), wide, wide),
        check_vma=False,
    )
```

```python
import functools
import math

import jax
import jax.numpy as jnp
from jax import lax
from jax.experimental import pallas as pl
from jax.experimental.pallas import tpu as pltpu
from jax.sharding import PartitionSpec as P

MESH = pl.DeviceIdType.MESH
F32 = jnp.float32
BF16 = jnp.bfloat16
NT = (((1,), (1,)), ((), ()))
NN = (((1,), (0,)), ((), ()))
TN = (((0,), (0,)), ((), ()))
NZ, NX, NY = 8, 4, 8
BLK = 64
DEAD = -64

FAMILIES = (
    ("right", 16), ("left", 16), ("pair", 16),
    ("table_z", 8), ("tile_z", 8), ("table_x", 24), ("tile_x", 24),
    ("part", 8), ("cr", 16), ("cl", 16), ("crx", 4), ("clx", 4), ("gx", 24), ("gz", 8),
)
BASE = {}
TOTAL = 0
for family, amount in FAMILIES:
    BASE[family] = TOTAL
    TOTAL += amount


def gelu_pair(hidden):
    inner = 0.7978845608028654 * (hidden + 0.044715 * hidden * hidden * hidden)
    tanh_term = jnp.tanh(inner)
    gelu_out = 0.5 * hidden * (1.0 + tanh_term)
    gelu_slope = 0.5 * (1.0 + tanh_term) + 0.5 * hidden * (
        1.0 - tanh_term * tanh_term
    ) * 0.7978845608028654 * (1.0 + 3.0 * 0.044715 * hidden * hidden)
    return (gelu_out, gelu_slope)


def place_in_order(row, y, core):
    dy = (row // 4 - y + NY) % NY
    other = jnp.where((row // 2) % 2 == core, 0, 1)
    near = jnp.minimum(dy, NY - dy)
    inner = 4 * near - 2 + 2 * other + jnp.where(dy > 4, 1, 0)
    return jnp.where(dy == 0, other, jnp.where(dy == 4, 14 + other, inner))


def kernel(
    scale, tok, cot, w1, w2, coord1, count1, coord2, count2, ig, g1, g2,
    w1v, w2v, c1, n1, c2, n2, xc, wall, mall, a1, a2, hid, ups, act, grd, part, psib, ssum, rbr, rbl, rbx,
    gr, xr, zs, zr, mv, dv, ms, md, send_sems, recv_sems, local_sems,
):
    row, col = lax.axis_index("row"), lax.axis_index("col")
    z, x, y, core = row // NX, row % NX, col // 2, col % 2

    def dev(dz=0, dx=0, dy=0, other=False):
        there = (1 - core) if other else core
        return ((z + dz) % NZ * NX + (x + dx) % NX, (y + dy) % NY * 2 + there)

    sibling = dev(other=True)
    right, left = dev(dy=1), dev(dy=NY - 1)
    z_right, z_left = dev(dz=1), dev(dz=NZ - 1)

    barrier = pltpu.get_barrier_semaphore()
    right_other, left_other = dev(dy=1, other=True), dev(dy=NY - 1, other=True)
    partners = [sibling, right, left, right_other, left_other]
    partners += [dev(dx=e) for e in range(1, NX)]
    partners += [dev(dz=e) for e in range(1, NZ)]
    for partner in partners:
        pl.semaphore_signal(barrier, inc=1, device_id=partner, device_id_type=MESH)

    loads = [
        pltpu.make_async_copy(src, dst, local_sems.at[n])
        for n, (src, dst) in enumerate((
            (w1, w1v), (w2, w2v), (coord1, c1), (count1, n1), (coord2, c2), (count2, n2),
            (tok, xc.at[col, 0]), (cot, xc.at[col, 1]),
        ))
    ]
    for load in loads:
        load.start()

    pending = []

    def describe(family, n, src, dst, target):
        slot = BASE[family] + n
        return pltpu.make_async_remote_copy(
            src_ref=src, dst_ref=dst, send_sem=send_sems.at[slot], recv_sem=recv_sems.at[slot],
            device_id=target, device_id_type=MESH,
        )

    def send(family, n, src, dst, target):
        copy = describe(family, n, src, dst, target)
        copy.start()
        pending.append(copy)

    def arrived(family, n, dst):
        describe(family, n, dst, dst, sibling).wait_recv()

    def shard(dy, other=False):
        return (y + dy) % NY * 2 + ((1 - core) if other else core)

    def plane(dz):
        return (z + dz) % NZ

    def piece(ref, j, h):
        return ref.at[j, pl.ds(64 * h, 64)]

    pl.semaphore_wait(barrier, len(partners))
    for j, own in ((0, tok), (1, cot)):
        for h in range(2):
            there = piece(xc.at[col], j, h)
            send("right", 2 * j + h, own.at[pl.ds(64 * h, 64)], there, right)
            send("left", 2 * j + h, own.at[pl.ds(64 * h, 64)], there, left)

    lane = lax.broadcasted_iota(jnp.int32, (1, 128), 1)
    low = lane < BLK
    for load in loads[:6]:
        load.wait()
    for k in range(2):
        wall[z, x, pl.ds(BLK * k, BLK), :] = jnp.concatenate(
            [w1v[k].astype(F32).T, w2v[k].astype(F32)], axis=1
        ).astype(BF16)
    hidden_places = [c1[0, 1], c1[1, 1], c2[0, 0], c2[1, 0]]
    model_places = [
        jnp.where(0 < n1[0, 0], c1[0, 0], DEAD), jnp.where(1 < n1[0, 0], c1[1, 0], DEAD),
        jnp.where(0 < n2[0, 0], c2[0, 1], DEAD), jnp.where(1 < n2[0, 0], c2[1, 1], DEAD),
    ]
    lane8 = lax.broadcasted_iota(jnp.int32, (8, 128), 1)
    line8 = lax.broadcasted_iota(jnp.int32, (8, 128), 0)
    meta = jnp.zeros((8, 128), jnp.int32)
    for n in range(4):
        meta = jnp.where((line8 == 0) & (lane8 == n), hidden_places[n], meta)
        meta = jnp.where(line8 == 1 + n, model_places[n], meta)
    mall[row] = meta

    def along_x(dz):
        there = plane(dz)
        for e in range(1, NX):
            at = mall.at[there * NX + x]
            send("table_x", 3 * dz + e - 1, at, at, dev(dx=e))
        for e in range(1, NX):
            at = wall.at[there, x]
            send("tile_x", 3 * dz + e - 1, at, at, dev(dx=e))

    for e in (1, 7, 2, 6, 3, 5, 4):
        send("table_z", e, mall.at[row], mall.at[row], dev(dz=e))
        send("tile_z", e, wall.at[z, x], wall.at[z, x], dev(dz=e))
    along_x(0)

    def planes_in(*away):
        for dz in away:
            arrived("table_z", NZ - dz, mall.at[plane(dz) * NX + x])
            arrived("tile_z", NZ - dz, wall.at[plane(dz), x])
            along_x(dz)

    def tables_in(*away):
        for dz in away:
            for e in range(1, NX):
                arrived("table_x", 3 * dz + e - 1, mall.at[plane(dz) * NX + (x + NX - e) % NX])

    def tiles_in(*away):
        for dz in away:
            for e in range(1, NX):
                arrived("tile_x", 3 * dz + e - 1, wall.at[plane(dz), (x + NX - e) % NX])

    hid[0] = jnp.zeros((BLK, 128), F32)
    ups[0] = jnp.zeros((BLK, 128), F32)
    for load in loads[6:]:
        load.wait()
    for j, own in ((0, tok), (1, cot)):
        send("pair", j, own, xc.at[col, j], sibling)

    def acts_in(d, j, h):
        n = 4 * (d - 1) + 2 * j + h
        if d <= 3 or j == 0:
            back = piece(xc.at[shard(NY - d)], j, h)
            arrived("right", n, back)
            if d < 3 or (d == 3 and j == 0):
                send("right", n + 4, back, back, right)
        if d <= 3 or j == 1:
            ahead = piece(xc.at[shard(d)], j, h)
            arrived("left", n, ahead)
            if d < 3 or (d == 3 and j == 1):
                send("left", n + 4, ahead, ahead, left)
        if h == 1:
            if d <= 3 or j == 0:
                whole = xc.at[shard(NY - d), j]
                send("pair", 2 * (NY - d) + j, whole, whole, sibling)
            if d <= 3 or j == 1:
                whole = xc.at[shard(d), j]
                send("pair", 2 * d + j, whole, whole, sibling)

    def places(c, matrix):
        found = []
        for i in range(2):
            for k in range(2):
                place = mall[2 * c + i, pl.ds(1 + 2 * matrix + k, 1), :] + 3 * i
                found.append([(jnp.where(low, 0, 1) + 2 * t) == place for t in range(3)])
        return found

    def build(c):
        ones, twos = places(c, 0), places(c, 1)
        for i in range(2):
            pack = wall[c // 2, (c % 2) * 2 + i].astype(F32)
            turned = pltpu.roll(pack, BLK, 1)
            first = jnp.where(low, pack, turned)
            second = jnp.where(low, turned, pack)
            for k in range(2):
                n = 2 * i + k
                here = slice(BLK * k, BLK * (k + 1))
                for t in range(3):
                    span = pl.ds(128 * t, 128)
                    a1[c, pl.ds(BLK * n, BLK), span] = jnp.where(ones[n][t], first[here], 0.0).astype(BF16)
                    a2[c, pl.ds(BLK * n, BLK), span] = jnp.where(twos[n][t], second[here], 0.0).astype(BF16)

    def build_planes(*away):
        for dz in away:
            there = plane(dz)

            def one_core(cc, carry, there=there):
                build(2 * there + cc)
                return carry

            lax.fori_loop(0, 2, one_core, 0)

    weights, sums = (a1, a2), (hid, ups)

    def forward_near(d, arrays, others):
        todo = []
        for other in others:
            for s, dy in enumerate(sorted({d, (NY - d) % NY})):
                place = {0: other, 4: 14 + other}.get(d, 4 * d - 2 + 2 * other + s)
                for j in arrays:
                    if other:
                        arrived("pair", 2 * dy + j, xc.at[shard(dy, True), j])
                    todo.append((j, shard(dy, other), place))
        for j, c, place in todo:
            product = lax.dot_general(weights[j][c], xc[c, j], NT, preferred_element_type=F32)
            sums[j][pl.ds(1 + 4 * place, 4)] = product.reshape(4, BLK, 128)
        for j, c, place in todo:
            for n in range(4):
                earlier = md[2 * c + n // 2, 2 * j + n % 2]
                at = 1 + 4 * place + n
                sums[j][at] = sums[j][at] + sums[j][earlier]

    def sort_slots():
        table = mall[:, 0, :]
        mv[...] = table
        rows = lax.broadcasted_iota(jnp.int32, (32, 128), 0)
        lanes = lax.broadcasted_iota(jnp.int32, (32, 128), 1)
        by_lane = 4 * place_in_order(lanes // 2, y, core) + lanes % 4
        by_row = 4 * place_in_order(rows, y, core) + 2 * (rows % 2)
        derived = jnp.zeros((32, 128), jnp.int32)
        for matrix, first in ((0, 0), (1, 2)):
            cols = [
                jnp.sum(jnp.where(lanes == first + k, table, 0), axis=1, keepdims=True) for k in range(2)
            ]
            flat = jnp.sum(
                jnp.where(rows == lanes // 2, jnp.where(lanes % 2 == 0, cols[0], cols[1]), 0),
                axis=0, keepdims=True,
            )
            for k in range(2):
                same = (flat == cols[k]) & (by_lane < by_row + k) & (lanes < 64)
                before = jnp.max(jnp.where(same, by_lane + 1, 0), axis=1, keepdims=True)
                derived = jnp.where(lanes == 2 * matrix + k, before, derived)
            ends = jnp.max(
                jnp.where((flat == rows) & (lanes < 64), by_lane + 1, 0), axis=1, keepdims=True
            )
            derived = jnp.where(lanes == 4 + matrix, ends, derived)
        dv[...] = derived
        copies = [
            pltpu.make_async_copy(mv, ms, local_sems.at[0]),
            pltpu.make_async_copy(dv, md, local_sems.at[1]),
        ]
        for copy in copies:
            copy.start()
        for copy in copies:
            copy.wait()

    planes_in(1, 7)
    acts_in(1, 0, 0)
    acts_in(1, 0, 1)
    planes_in(2, 6)
    acts_in(1, 1, 0)
    acts_in(1, 1, 1)
    acts_in(2, 0, 0)
    planes_in(3, 5)
    acts_in(2, 0, 1)
    planes_in(4)
    tables_in(0, 1, 7)
    tiles_in(0, 1, 7)
    build_planes(0, 1, 7)
    acts_in(2, 1, 0)
    acts_in(2, 1, 1)
    tables_in(2, 6)
    tiles_in(2, 6)
    build_planes(2, 6)
    acts_in(3, 0, 0)
    tables_in(3, 5, 4)
    sort_slots()
    acts_in(3, 0, 1)
    acts_in(3, 1, 0)
    tiles_in(3, 5, 4)
    build_planes(3, 5, 4)
    acts_in(3, 1, 1)
    forward_near(0, (0, 1), (0, 1))
    forward_near(1, (0,), (0, 1))
    forward_near(1, (1,), (0, 1))
    acts_in(4, 0, 0)
    acts_in(4, 1, 0)
    forward_near(2, (0,), (0, 1))
    forward_near(2, (1,), (0, 1))
    acts_in(4, 0, 1)
    acts_in(4, 1, 1)
    forward_near(3, (0,), (0, 1))
    forward_near(3, (1,), (0, 1))
    forward_near(4, (0, 1), (0,))
    forward_near(4, (0, 1), (1,))

    def middle(q, carry):
        gelu_out, gelu_slope = gelu_pair(hid[md[q, 4]])
        act[q] = gelu_out.astype(BF16)
        grd[q] = (ups[md[q, 5]] * gelu_slope).astype(BF16)
        return carry

    lax.fori_loop(0, 24, middle, 0)

    def pick(product, found):
        total = jnp.where(found[0], product[:, 0:128], 0.0)
        for t in range(1, 3):
            total = total + jnp.where(found[t], product[:, 128 * t : 128 * (t + 1)], 0.0)
        return total + pltpu.roll(total, BLK, 1)

    def chosen(source, c, first):
        return jnp.concatenate([source[ms[2 * c + n // 2, first + n % 2]] for n in range(4)], axis=0)

    def to_input(c):
        part[c] = lax.dot_general(
            chosen(grd, c, 0), a1[c], TN, preferred_element_type=F32
        ).astype(BF16)

    def to_blocks(c):
        ones, twos = places(c, 0), places(c, 1)
        one = lax.dot_general(chosen(grd, c, 0), xc[c, 0], NN, preferred_element_type=F32)
        two = lax.dot_general(chosen(act, c, 2), xc[c, 1], NN, preferred_element_type=F32)
        for n in range(4):
            span = slice(BLK * n, BLK * (n + 1))
            both = jnp.where(low, pick(one[span], ones[n]), pick(two[span], twos[n]))
            gr[c // 2, (c % 2) * 2 + n // 2, pl.ds(BLK * (n % 2), BLK), :] = both.astype(BF16)

    def quarter(ref, q):
        return ref.at[pl.ds(32 * q, 32)]

    def settle(dy, *quarters):
        there = (y + dy) % NY
        for q in quarters:
            rows = pl.ds(32 * q, 32)
            total = part[shard(dy), rows].astype(F32) + psib[there, rows].astype(F32)
            if dy == 0:
                for family, buffer in (("cr", rbr), ("cl", rbl)):
                    arrived(family, 12 + q, quarter(buffer.at[3], q))
                    total = total + buffer[3, rows].astype(F32)
                ig[rows, :] = total
                continue
            chain, step = (0, 4 - dy) if dy < 4 else (1, dy - 4)
            family, buffer, target = (("cr", rbr, right), ("cl", rbl, left))[chain]
            if step > 1 or q // 2 == chain:
                arrived(family, 4 * step - 4 + q, quarter(buffer.at[step - 1], q))
                total = total + buffer[step - 1, rows].astype(F32)
            if step == 1 and q // 2 == chain:
                arrived(family + "x", q, quarter(rbx, q))
                total = total + rbx[rows].astype(F32)
            ssum[there, rows] = total.astype(BF16)
            send(family, 4 * step + q, quarter(ssum.at[there], q), quarter(buffer.at[step], q), target)

    def opening():
        for q in (0, 2, 1, 3):
            family, buffer, target, target_other = (
                ("cr", rbr, right, right_other), ("cl", rbl, left, left_other)
            )[q // 2]
            send(family, q, quarter(part.at[shard(4)], q), quarter(buffer.at[0], q), target)
            send(family + "x", q, quarter(part.at[shard(4, True)], q), quarter(rbx, q), target_other)

    def paired(*away):
        for dy in away:
            arrived("part", dy, psib.at[(y + dy) % NY])

    def plane_sum(dz):
        total = gr[plane(dz), x].astype(F32)
        for e in range(1, NX):
            arrived("gx", dz * 3 + e - 1, xr.at[dz, e - 1])
            total = total + xr[dz, e - 1].astype(F32)
        return total

    def plane_on(*away):
        for dz in away:
            zs[dz] = plane_sum(dz).astype(BF16)
            send("gz", dz, zs.at[dz], zr.at[dz], dev(dz=dz))

    def inputs_step(dy):
        there = (y + dy) % NY
        for other in (True, False):
            to_input(shard(dy, other))
            if other and dy != 4:
                send("part", dy, part.at[shard(dy, True)], psib.at[there], sibling)

    def blocks_step(dz):
        there = plane(dz)
        for cc in range(2):
            to_blocks(there * 2 + cc)
        for e in range(1, NX):
            send("gx", dz * 3 + e - 1, gr.at[there, (x + e) % NX], xr.at[dz, e - 1], dev(dx=e))

    inputs_step(4)
    opening()
    blocks_step(4)
    inputs_step(3)
    inputs_step(5)
    blocks_step(3)
    blocks_step(5)
    inputs_step(2)
    inputs_step(6)
    blocks_step(2)
    paired(3, 5)
    settle(3, 2, 3)
    settle(5, 0, 1)
    blocks_step(6)
    inputs_step(1)
    inputs_step(7)
    blocks_step(1)
    blocks_step(7)
    inputs_step(0)
    blocks_step(0)
    plane_on(4)
    for n in range(2):
        settle(3, n)
        settle(5, 2 + n)
    plane_on(3)
    paired(2, 6)
    for n in range(2):
        settle(2, 2 + n)
        settle(6, n)
    plane_on(5)
    for n in range(2):
        settle(2, n)
        settle(6, 2 + n)
    plane_on(2)
    paired(1, 7)
    for n in range(2):
        settle(1, 2 + n)
        settle(7, n)
    plane_on(6)
    for n in range(2):
        settle(1, n)
        settle(7, 2 + n)
    plane_on(1)
    plane_on(7)
    paired(0)
    settle(0, 2, 3, 0, 1)
    total = plane_sum(0)
    for e in range(1, NZ):
        arrived("gz", e, zr.at[e])
        total = total + zr[e].astype(F32)
    total = total * scale
    for k in range(2):
        here = slice(BLK * k, BLK * (k + 1))
        g1[k] = total[here, 0:BLK].T
        g2[k] = total[here, BLK:128]

    for copy in pending:
        copy.wait_send()


def finish(ig, g1, g2, input_grad, grad_one, grad_two, sems):
    copies = [
        pltpu.make_async_copy(src, dst, sems.at[n])
        for n, (src, dst) in enumerate(((ig, input_grad), (g1, grad_one), (g2, grad_two)))
    ]
    for copy in copies:
        copy.start()
    for copy in copies:
        copy.wait()


def shards(tokens, cotangent, w1_blocks, w1_coords, w1_count, w2_blocks, w2_coords, w2_count):
    scale = 1.0 / math.sqrt(4096)
    shard = (128, 384)
    blocks = (2, BLK, BLK)
    anywhere = pl.BlockSpec(memory_space=pl.ANY)
    results = (
        jax.ShapeDtypeStruct(shard, F32),
        jax.ShapeDtypeStruct(blocks, F32),
        jax.ShapeDtypeStruct(blocks, F32),
    )
    vmem = pl.BlockSpec(memory_space=pltpu.VMEM)
    tokens, cotangent, w1_in, w2_in, c1_in, c2_in = [
        pltpu.with_memory_space_constraint(array, pltpu.HBM)
        for array in (
            tokens, cotangent, w1_blocks.reshape(blocks), w2_blocks.reshape(blocks),
            w1_coords.reshape(2, 2), w2_coords.reshape(2, 2),
        )
    ]
    halfway = pl.pallas_call(
        functools.partial(kernel, scale),
        out_shape=tuple(pltpu.VMEM(result.shape, F32) for result in results),
        in_specs=[anywhere] * 8,
        out_specs=(vmem,) * 3,
        scratch_shapes=[
            pltpu.VMEM(blocks, BF16),
            pltpu.VMEM(blocks, BF16),
            pltpu.SMEM((2, 2), jnp.int32),
            pltpu.SMEM((1, 1), jnp.int32),
            pltpu.SMEM((2, 2), jnp.int32),
            pltpu.SMEM((1, 1), jnp.int32),
            pltpu.VMEM((16, 2) + shard, BF16),
            pltpu.VMEM((NZ, NX, 128, 128), BF16),
            pltpu.VMEM((32, 8, 128), jnp.int32),
            pltpu.VMEM((16, 256, 384), BF16),
            pltpu.VMEM((16, 256, 384), BF16),
            pltpu.VMEM((65, BLK, 128), F32),
            pltpu.VMEM((65, BLK, 128), F32),
            pltpu.VMEM((24, BLK, 128), BF16),
            pltpu.VMEM((24, BLK, 128), BF16),
            pltpu.VMEM((16,) + shard, BF16),
            pltpu.VMEM((8,) + shard, BF16),
            pltpu.VMEM((8,) + shard, BF16),
            pltpu.VMEM((4,) + shard, BF16),
            pltpu.VMEM((4,) + shard, BF16),
            pltpu.VMEM(shard, BF16),
            pltpu.VMEM((NZ, NX, 128, 128), BF16),
            pltpu.VMEM((NZ, 3, 128, 128), BF16),
            pltpu.VMEM((NZ, 128, 128), BF16),
            pltpu.VMEM((NZ, 128, 128), BF16),
            pltpu.VMEM((32, 128), jnp.int32),
            pltpu.VMEM((32, 128), jnp.int32),
            pltpu.SMEM((32, 128), jnp.int32),
            pltpu.SMEM((32, 128), jnp.int32),
            pltpu.SemaphoreType.DMA((TOTAL,)),
            pltpu.SemaphoreType.DMA((TOTAL,)),
            pltpu.SemaphoreType.DMA((8,)),
        ],
        compiler_params=pltpu.CompilerParams(
            collective_id=0, has_side_effects=True, vmem_limit_bytes=48 * 1024 * 1024
        ),
        cost_estimate=pl.CostEstimate(
            flops=16 * 5 * 2 * 256 * 384 * 128, bytes_accessed=1 << 20, transcendentals=24 * 64 * 128
        ),
    )(tokens, cotangent, w1_in, w2_in, c1_in, w1_count, c2_in, w2_count)
    input_grad, grad_one, grad_two = pl.pallas_call(
        finish,
        out_shape=results,
        in_specs=[vmem] * 3,
        out_specs=(anywhere,) * 3,
        scratch_shapes=[pltpu.SemaphoreType.DMA((3,))],
    )(*[pltpu.with_memory_space_constraint(array, pltpu.VMEM) for array in halfway])
    return (input_grad, grad_one.reshape(w1_blocks.shape), grad_two.reshape(w2_blocks.shape))


def solution(mesh):
    wide = P("row", "col", None, None, None)
    return jax.shard_map(
        shards,
        mesh=mesh,
        in_specs=(
            P("row", "col"), P("row", "col"),
            wide, P("row", "col", None, None), P("row", "col"),
            wide, P("row", "col", None, None), P("row", "col"),
        ),
        out_specs=(P("row", "col"), wide, wide),
        check_vma=False,
    )
```

```python
import functools
import math

import jax
import jax.numpy as jnp
from jax import lax
from jax.experimental import pallas as pl
from jax.experimental.pallas import tpu as pltpu
from jax.sharding import PartitionSpec as P

MESH = pl.DeviceIdType.MESH
F32 = jnp.float32
BF16 = jnp.bfloat16
NT = (((1,), (1,)), ((), ()))
NN = (((1,), (0,)), ((), ()))
TN = (((0,), (0,)), ((), ()))
NZ, NX, NY = 8, 4, 8
BLK = 64
DEAD = -64

FAMILIES = (
    ("right", 16), ("left", 16), ("pair", 16),
    ("table_z", 8), ("tile_z", 8), ("table_x", 24), ("tile_x", 24),
    ("part", 8), ("cr", 16), ("cl", 16), ("crx", 4), ("clx", 4), ("gx", 24), ("gz", 8),
)
BASE = {}
TOTAL = 0
for family, amount in FAMILIES:
    BASE[family] = TOTAL
    TOTAL += amount


def gelu_pair(hidden):
    inner = 0.7978845608028654 * (hidden + 0.044715 * hidden * hidden * hidden)
    tanh_term = jnp.tanh(inner)
    gelu_out = 0.5 * hidden * (1.0 + tanh_term)
    gelu_slope = 0.5 * (1.0 + tanh_term) + 0.5 * hidden * (
        1.0 - tanh_term * tanh_term
    ) * 0.7978845608028654 * (1.0 + 3.0 * 0.044715 * hidden * hidden)
    return (gelu_out, gelu_slope)


def place_in_order(row, y, core):
    dy = (row // 4 - y + NY) % NY
    other = jnp.where((row // 2) % 2 == core, 0, 1)
    near = jnp.minimum(dy, NY - dy)
    inner = 4 * near - 2 + 2 * other + jnp.where(dy > 4, 1, 0)
    return jnp.where(dy == 0, other, jnp.where(dy == 4, 14 + other, inner))


def kernel(
    scale, tok, cot, w1, w2, coord1, count1, coord2, count2, ig, g1, g2,
    w1v, w2v, c1, n1, c2, n2, xc, wall, mall, a1, a2, hid, ups, act, grd, part, psib, ssum, rbr, rbl, rbx,
    gr, xr, zs, zr, mv, dv, ms, md, send_sems, recv_sems, local_sems,
):
    row, col = lax.axis_index("row"), lax.axis_index("col")
    z, x, y, core = row // NX, row % NX, col // 2, col % 2

    def dev(dz=0, dx=0, dy=0, other=False):
        there = (1 - core) if other else core
        return ((z + dz) % NZ * NX + (x + dx) % NX, (y + dy) % NY * 2 + there)

    sibling = dev(other=True)
    right, left = dev(dy=1), dev(dy=NY - 1)
    z_right, z_left = dev(dz=1), dev(dz=NZ - 1)

    barrier = pltpu.get_barrier_semaphore()
    right_other, left_other = dev(dy=1, other=True), dev(dy=NY - 1, other=True)
    partners = [sibling, right, left, right_other, left_other]
    partners += [dev(dx=e) for e in range(1, NX)]
    partners += [dev(dz=e) for e in range(1, NZ)]
    for partner in partners:
        pl.semaphore_signal(barrier, inc=1, device_id=partner, device_id_type=MESH)

    loads = [
        pltpu.make_async_copy(src, dst, local_sems.at[n])
        for n, (src, dst) in enumerate((
            (w1, w1v), (w2, w2v), (coord1, c1), (count1, n1), (coord2, c2), (count2, n2),
            (tok, xc.at[col, 0]), (cot, xc.at[col, 1]),
        ))
    ]
    for load in loads:
        load.start()

    pending = []

    def describe(family, n, src, dst, target):
        slot = BASE[family] + n
        return pltpu.make_async_remote_copy(
            src_ref=src, dst_ref=dst, send_sem=send_sems.at[slot], recv_sem=recv_sems.at[slot],
            device_id=target, device_id_type=MESH,
        )

    def send(family, n, src, dst, target):
        copy = describe(family, n, src, dst, target)
        copy.start()
        pending.append(copy)

    def arrived(family, n, dst):
        describe(family, n, dst, dst, sibling).wait_recv()

    def shard(dy, other=False):
        return (y + dy) % NY * 2 + ((1 - core) if other else core)

    def plane(dz):
        return (z + dz) % NZ

    def piece(ref, j, h):
        return ref.at[j, pl.ds(64 * h, 64)]

    pl.semaphore_wait(barrier, len(partners))
    for j, own in ((0, tok), (1, cot)):
        for h in range(2):
            there = piece(xc.at[col], j, h)
            send("right", 2 * j + h, own.at[pl.ds(64 * h, 64)], there, right)
            send("left", 2 * j + h, own.at[pl.ds(64 * h, 64)], there, left)

    lane = lax.broadcasted_iota(jnp.int32, (1, 128), 1)
    low = lane < BLK
    for load in loads[:6]:
        load.wait()
    for k in range(2):
        wall[z, x, pl.ds(BLK * k, BLK), :] = jnp.concatenate(
            [w1v[k].astype(F32).T, w2v[k].astype(F32)], axis=1
        ).astype(BF16)
    hidden_places = [c1[0, 1], c1[1, 1], c2[0, 0], c2[1, 0]]
    model_places = [
        jnp.where(0 < n1[0, 0], c1[0, 0], DEAD), jnp.where(1 < n1[0, 0], c1[1, 0], DEAD),
        jnp.where(0 < n2[0, 0], c2[0, 1], DEAD), jnp.where(1 < n2[0, 0], c2[1, 1], DEAD),
    ]
    lane8 = lax.broadcasted_iota(jnp.int32, (8, 128), 1)
    line8 = lax.broadcasted_iota(jnp.int32, (8, 128), 0)
    meta = jnp.zeros((8, 128), jnp.int32)
    for n in range(4):
        meta = jnp.where((line8 == 0) & (lane8 == n), hidden_places[n], meta)
        meta = jnp.where(line8 == 1 + n, model_places[n], meta)
    mall[row] = meta

    def along_x(dz):
        there = plane(dz)
        for e in range(1, NX):
            at = mall.at[there * NX + x]
            send("table_x", 3 * dz + e - 1, at, at, dev(dx=e))
        for e in range(1, NX):
            at = wall.at[there, x]
            send("tile_x", 3 * dz + e - 1, at, at, dev(dx=e))

    for e in (1, 7, 2, 6, 3, 5, 4):
        send("table_z", e, mall.at[row], mall.at[row], dev(dz=e))
        send("tile_z", e, wall.at[z, x], wall.at[z, x], dev(dz=e))
    along_x(0)

    def planes_in(*away):
        for dz in away:
            arrived("table_z", NZ - dz, mall.at[plane(dz) * NX + x])
            arrived("tile_z", NZ - dz, wall.at[plane(dz), x])
            along_x(dz)

    def tables_in(*away):
        for dz in away:
            for e in range(1, NX):
                arrived("table_x", 3 * dz + e - 1, mall.at[plane(dz) * NX + (x + NX - e) % NX])

    def tiles_in(*away):
        for dz in away:
            for e in range(1, NX):
                arrived("tile_x", 3 * dz + e - 1, wall.at[plane(dz), (x + NX - e) % NX])

    hid[0] = jnp.zeros((BLK, 128), F32)
    ups[0] = jnp.zeros((BLK, 128), F32)
    for load in loads[6:]:
        load.wait()
    for j, own in ((0, tok), (1, cot)):
        send("pair", j, own, xc.at[col, j], sibling)

    def acts_in(d, j, h):
        n = 4 * (d - 1) + 2 * j + h
        if d <= 3 or j == 0:
            back = piece(xc.at[shard(NY - d)], j, h)
            arrived("right", n, back)
            if d < 3 or (d == 3 and j == 0):
                send("right", n + 4, back, back, right)
        if d <= 3 or j == 1:
            ahead = piece(xc.at[shard(d)], j, h)
            arrived("left", n, ahead)
            if d < 3 or (d == 3 and j == 1):
                send("left", n + 4, ahead, ahead, left)
        if h == 1:
            if d <= 3 or j == 0:
                whole = xc.at[shard(NY - d), j]
                send("pair", 2 * (NY - d) + j, whole, whole, sibling)
            if d <= 3 or j == 1:
                whole = xc.at[shard(d), j]
                send("pair", 2 * d + j, whole, whole, sibling)

    def places(c, matrix):
        found = []
        for i in range(2):
            for k in range(2):
                place = mall[2 * c + i, pl.ds(1 + 2 * matrix + k, 1), :] + 3 * i
                found.append([(jnp.where(low, 0, 1) + 2 * t) == place for t in range(3)])
        return found

    def build(c):
        ones, twos = places(c, 0), places(c, 1)
        for i in range(2):
            pack = wall[c // 2, (c % 2) * 2 + i].astype(F32)
            turned = pltpu.roll(pack, BLK, 1)
            first = jnp.where(low, pack, turned)
            second = jnp.where(low, turned, pack)
            for k in range(2):
                n = 2 * i + k
                here = slice(BLK * k, BLK * (k + 1))
                for t in range(3):
                    span = pl.ds(128 * t, 128)
                    a1[c, pl.ds(BLK * n, BLK), span] = jnp.where(ones[n][t], first[here], 0.0).astype(BF16)
                    a2[c, pl.ds(BLK * n, BLK), span] = jnp.where(twos[n][t], second[here], 0.0).astype(BF16)

    def build_planes(*away):
        for dz in away:
            there = plane(dz)

            def one_core(cc, carry, there=there):
                build(2 * there + cc)
                return carry

            lax.fori_loop(0, 2, one_core, 0)

    weights, sums = (a1, a2), (hid, ups)

    def forward_near(d, arrays, others):
        todo = []
        for other in others:
            for s, dy in enumerate(sorted({d, (NY - d) % NY})):
                place = {0: other, 4: 14 + other}.get(d, 4 * d - 2 + 2 * other + s)
                for j in arrays:
                    if other:
                        arrived("pair", 2 * dy + j, xc.at[shard(dy, True), j])
                    todo.append((j, shard(dy, other), place))
        for j, c, place in todo:
            product = lax.dot_general(weights[j][c], xc[c, j], NT, preferred_element_type=F32)
            sums[j][pl.ds(1 + 4 * place, 4)] = product.reshape(4, BLK, 128)
        for j, c, place in todo:
            for n in range(4):
                earlier = md[2 * c + n // 2, 2 * j + n % 2]
                at = 1 + 4 * place + n
                sums[j][at] = sums[j][at] + sums[j][earlier]

    def sort_slots():
        table = mall[:, 0, :]
        mv[...] = table
        rows = lax.broadcasted_iota(jnp.int32, (32, 128), 0)
        lanes = lax.broadcasted_iota(jnp.int32, (32, 128), 1)
        by_lane = 4 * place_in_order(lanes // 2, y, core) + lanes % 4
        by_row = 4 * place_in_order(rows, y, core) + 2 * (rows % 2)
        derived = jnp.zeros((32, 128), jnp.int32)
        for matrix, first in ((0, 0), (1, 2)):
            cols = [
                jnp.sum(jnp.where(lanes == first + k, table, 0), axis=1, keepdims=True) for k in range(2)
            ]
            flat = jnp.sum(
                jnp.where(rows == lanes // 2, jnp.where(lanes % 2 == 0, cols[0], cols[1]), 0),
                axis=0, keepdims=True,
            )
            for k in range(2):
                same = (flat == cols[k]) & (by_lane < by_row + k) & (lanes < 64)
                before = jnp.max(jnp.where(same, by_lane + 1, 0), axis=1, keepdims=True)
                derived = jnp.where(lanes == 2 * matrix + k, before, derived)
            ends = jnp.max(
                jnp.where((flat == rows) & (lanes < 64), by_lane + 1, 0), axis=1, keepdims=True
            )
            derived = jnp.where(lanes == 4 + matrix, ends, derived)
        dv[...] = derived
        copies = [
            pltpu.make_async_copy(mv, ms, local_sems.at[0]),
            pltpu.make_async_copy(dv, md, local_sems.at[1]),
        ]
        for copy in copies:
            copy.start()
        for copy in copies:
            copy.wait()

    planes_in(1, 7)
    acts_in(1, 0, 0)
    acts_in(1, 0, 1)
    planes_in(2, 6)
    acts_in(1, 1, 0)
    acts_in(1, 1, 1)
    acts_in(2, 0, 0)
    planes_in(3, 5)
    acts_in(2, 0, 1)
    planes_in(4)
    tables_in(0, 1, 7)
    tiles_in(0, 1, 7)
    build_planes(0, 1, 7)
    acts_in(2, 1, 0)
    acts_in(2, 1, 1)
    tables_in(2, 6)
    tiles_in(2, 6)
    build_planes(2, 6)
    acts_in(3, 0, 0)
    tables_in(3, 5, 4)
    sort_slots()
    acts_in(3, 0, 1)
    acts_in(3, 1, 0)
    tiles_in(3, 5, 4)
    build_planes(3, 5, 4)
    acts_in(3, 1, 1)
    forward_near(0, (0, 1), (0, 1))
    forward_near(1, (0,), (0, 1))
    forward_near(1, (1,), (0, 1))
    acts_in(4, 0, 0)
    acts_in(4, 1, 0)
    forward_near(2, (0,), (0, 1))
    forward_near(2, (1,), (0, 1))
    acts_in(4, 0, 1)
    acts_in(4, 1, 1)
    forward_near(3, (0,), (0, 1))
    forward_near(3, (1,), (0, 1))
    forward_near(4, (0, 1), (0,))
    forward_near(4, (0, 1), (1,))

    def middle(q, carry):
        gelu_out, gelu_slope = gelu_pair(hid[md[q, 4]])
        act[q] = gelu_out.astype(BF16)
        grd[q] = (ups[md[q, 5]] * gelu_slope).astype(BF16)
        return carry

    lax.fori_loop(0, 24, middle, 0)

    def pick(product, found):
        total = jnp.where(found[0], product[:, 0:128], 0.0)
        for t in range(1, 3):
            total = total + jnp.where(found[t], product[:, 128 * t : 128 * (t + 1)], 0.0)
        return total + pltpu.roll(total, BLK, 1)

    def chosen(source, c, first):
        return jnp.concatenate([source[ms[2 * c + n // 2, first + n % 2]] for n in range(4)], axis=0)

    def to_input(c):
        part[c] = lax.dot_general(
            chosen(grd, c, 0), a1[c], TN, preferred_element_type=F32
        ).astype(BF16)

    def to_blocks(c):
        ones, twos = places(c, 0), places(c, 1)
        one = lax.dot_general(chosen(grd, c, 0), xc[c, 0], NN, preferred_element_type=F32)
        two = lax.dot_general(chosen(act, c, 2), xc[c, 1], NN, preferred_element_type=F32)
        for n in range(4):
            span = slice(BLK * n, BLK * (n + 1))
            both = jnp.where(low, pick(one[span], ones[n]), pick(two[span], twos[n]))
            gr[c // 2, (c % 2) * 2 + n // 2, pl.ds(BLK * (n % 2), BLK), :] = both.astype(BF16)

    def quarter(ref, q):
        return ref.at[pl.ds(32 * q, 32)]

    def settle(dy, *quarters):
        there = (y + dy) % NY
        for q in quarters:
            rows = pl.ds(32 * q, 32)
            total = part[shard(dy), rows].astype(F32) + psib[there, rows].astype(F32)
            if dy == 0:
                for family, buffer in (("cr", rbr), ("cl", rbl)):
                    arrived(family, 12 + q, quarter(buffer.at[3], q))
                    total = total + buffer[3, rows].astype(F32)
                ig[rows, :] = total
                continue
            chain, step = (0, 4 - dy) if dy < 4 else (1, dy - 4)
            family, buffer, target = (("cr", rbr, right), ("cl", rbl, left))[chain]
            if step > 1 or q // 2 == chain:
                arrived(family, 4 * step - 4 + q, quarter(buffer.at[step - 1], q))
                total = total + buffer[step - 1, rows].astype(F32)
            if step == 1 and q // 2 == chain:
                arrived(family + "x", q, quarter(rbx, q))
                total = total + rbx[rows].astype(F32)
            ssum[there, rows] = total.astype(BF16)
            send(family, 4 * step + q, quarter(ssum.at[there], q), quarter(buffer.at[step], q), target)

    def opening():
        for q in (0, 2, 1, 3):
            family, buffer, target, target_other = (
                ("cr", rbr, right, right_other), ("cl", rbl, left, left_other)
            )[q // 2]
            send(family, q, quarter(part.at[shard(4)], q), quarter(buffer.at[0], q), target)
            send(family + "x", q, quarter(part.at[shard(4, True)], q), quarter(rbx, q), target_other)

    def paired(*away):
        for dy in away:
            arrived("part", dy, psib.at[(y + dy) % NY])

    def plane_sum(dz):
        total = gr[plane(dz), x].astype(F32)
        for e in range(1, NX):
            arrived("gx", dz * 3 + e - 1, xr.at[dz, e - 1])
            total = total + xr[dz, e - 1].astype(F32)
        return total

    def plane_on(*away):
        for dz in away:
            zs[dz] = plane_sum(dz).astype(BF16)
            send("gz", dz, zs.at[dz], zr.at[dz], dev(dz=dz))

    def inputs_step(dy):
        there = (y + dy) % NY
        for other in (True, False):
            to_input(shard(dy, other))
            if other and dy != 4:
                send("part", dy, part.at[shard(dy, True)], psib.at[there], sibling)

    def blocks_step(dz):
        there = plane(dz)
        for cc in range(2):
            to_blocks(there * 2 + cc)
        for e in range(1, NX):
            send("gx", dz * 3 + e - 1, gr.at[there, (x + e) % NX], xr.at[dz, e - 1], dev(dx=e))

    inputs_step(4)
    opening()
    blocks_step(4)
    inputs_step(3)
    inputs_step(5)
    blocks_step(3)
    inputs_step(2)
    inputs_step(6)
    blocks_step(5)
    blocks_step(2)
    paired(3, 5)
    settle(3, 2, 3)
    settle(5, 0, 1)
    blocks_step(6)
    inputs_step(1)
    inputs_step(7)
    blocks_step(1)
    for n in range(2):
        settle(3, n)
        settle(5, 2 + n)
    blocks_step(7)
    inputs_step(0)
    blocks_step(0)
    plane_on(4)
    paired(2, 6)
    for n in range(2):
        settle(2, 2 + n)
        settle(6, n)
    plane_on(3)
    for n in range(2):
        settle(2, n)
        settle(6, 2 + n)
    plane_on(5)
    paired(1, 7)
    for n in range(2):
        settle(1, 2 + n)
        settle(7, n)
    plane_on(2)
    for n in range(2):
        settle(1, n)
        settle(7, 2 + n)
    plane_on(6)
    plane_on(1)
    paired(0)
    settle(0, 2, 3, 0, 1)
    plane_on(7)
    total = plane_sum(0)
    for e in range(1, NZ):
        arrived("gz", e, zr.at[e])
        total = total + zr[e].astype(F32)
    total = total * scale
    for k in range(2):
        here = slice(BLK * k, BLK * (k + 1))
        g1[k] = total[here, 0:BLK].T
        g2[k] = total[here, BLK:128]

    for copy in pending:
        copy.wait_send()


def finish(ig, g1, g2, input_grad, grad_one, grad_two, sems):
    copies = [
        pltpu.make_async_copy(src, dst, sems.at[n])
        for n, (src, dst) in enumerate(((ig, input_grad), (g1, grad_one), (g2, grad_two)))
    ]
    for copy in copies:
        copy.start()
    for copy in copies:
        copy.wait()


def shards(tokens, cotangent, w1_blocks, w1_coords, w1_count, w2_blocks, w2_coords, w2_count):
    scale = 1.0 / math.sqrt(4096)
    shard = (128, 384)
    blocks = (2, BLK, BLK)
    anywhere = pl.BlockSpec(memory_space=pl.ANY)
    results = (
        jax.ShapeDtypeStruct(shard, F32),
        jax.ShapeDtypeStruct(blocks, F32),
        jax.ShapeDtypeStruct(blocks, F32),
    )
    vmem = pl.BlockSpec(memory_space=pltpu.VMEM)
    tokens, cotangent, w1_in, w2_in, c1_in, c2_in = [
        pltpu.with_memory_space_constraint(array, pltpu.HBM)
        for array in (
            tokens, cotangent, w1_blocks.reshape(blocks), w2_blocks.reshape(blocks),
            w1_coords.reshape(2, 2), w2_coords.reshape(2, 2),
        )
    ]
    halfway = pl.pallas_call(
        functools.partial(kernel, scale),
        out_shape=tuple(pltpu.VMEM(result.shape, F32) for result in results),
        in_specs=[anywhere] * 8,
        out_specs=(vmem,) * 3,
        scratch_shapes=[
            pltpu.VMEM(blocks, BF16),
            pltpu.VMEM(blocks, BF16),
            pltpu.SMEM((2, 2), jnp.int32),
            pltpu.SMEM((1, 1), jnp.int32),
            pltpu.SMEM((2, 2), jnp.int32),
            pltpu.SMEM((1, 1), jnp.int32),
            pltpu.VMEM((16, 2) + shard, BF16),
            pltpu.VMEM((NZ, NX, 128, 128), BF16),
            pltpu.VMEM((32, 8, 128), jnp.int32),
            pltpu.VMEM((16, 256, 384), BF16),
            pltpu.VMEM((16, 256, 384), BF16),
            pltpu.VMEM((65, BLK, 128), F32),
            pltpu.VMEM((65, BLK, 128), F32),
            pltpu.VMEM((24, BLK, 128), BF16),
            pltpu.VMEM((24, BLK, 128), BF16),
            pltpu.VMEM((16,) + shard, BF16),
            pltpu.VMEM((8,) + shard, BF16),
            pltpu.VMEM((8,) + shard, BF16),
            pltpu.VMEM((4,) + shard, BF16),
            pltpu.VMEM((4,) + shard, BF16),
            pltpu.VMEM(shard, BF16),
            pltpu.VMEM((NZ, NX, 128, 128), BF16),
            pltpu.VMEM((NZ, 3, 128, 128), BF16),
            pltpu.VMEM((NZ, 128, 128), BF16),
            pltpu.VMEM((NZ, 128, 128), BF16),
            pltpu.VMEM((32, 128), jnp.int32),
            pltpu.VMEM((32, 128), jnp.int32),
            pltpu.SMEM((32, 128), jnp.int32),
            pltpu.SMEM((32, 128), jnp.int32),
            pltpu.SemaphoreType.DMA((TOTAL,)),
            pltpu.SemaphoreType.DMA((TOTAL,)),
            pltpu.SemaphoreType.DMA((8,)),
        ],
        compiler_params=pltpu.CompilerParams(
            collective_id=0, has_side_effects=True, vmem_limit_bytes=48 * 1024 * 1024
        ),
        cost_estimate=pl.CostEstimate(
            flops=16 * 5 * 2 * 256 * 384 * 128, bytes_accessed=1 << 20, transcendentals=24 * 64 * 128
        ),
    )(tokens, cotangent, w1_in, w2_in, c1_in, w1_count, c2_in, w2_count)
    input_grad, grad_one, grad_two = pl.pallas_call(
        finish,
        out_shape=results,
        in_specs=[vmem] * 3,
        out_specs=(anywhere,) * 3,
        scratch_shapes=[pltpu.SemaphoreType.DMA((3,))],
    )(*[pltpu.with_memory_space_constraint(array, pltpu.VMEM) for array in halfway])
    return (input_grad, grad_one.reshape(w1_blocks.shape), grad_two.reshape(w2_blocks.shape))


def solution(mesh):
    wide = P("row", "col", None, None, None)
    return jax.shard_map(
        shards,
        mesh=mesh,
        in_specs=(
            P("row", "col"), P("row", "col"),
            wide, P("row", "col", None, None), P("row", "col"),
            wide, P("row", "col", None, None), P("row", "col"),
        ),
        out_specs=(P("row", "col"), wide, wide),
        check_vma=False,
    )
```
